32 devices in a mesh: theta: 8 (over y, x, core), span: 4 (over z).
Axes of the slice: x: 2, y: 2, z: 4, core: 2. Of those that a mesh axis runs over, the one named last changes fastest.
Arguments:
- velocity: float32 [3, 9, 64, 8192], P(None, None, 'theta', 'span'), may hold values from -6 to 6
- pressure: float32 [9, 64, 8192], P(None, 'theta', 'span'), may hold values from -6 to 6
- diffusivity: float32 [64, 8192], P('theta', 'span'), may hold values from 0.3 to 3
- live_blocks: int32 [8, 4], P('theta', 'span'), may hold values from 1 to 8
- owner_map: int32 [64, 8192], P('theta', 'span'), may hold values from 0 to 511, as said below
- coarse_diag: float32 [16, 512], P('theta', 'span'), may hold values from 0.5 to 4
Outputs:
- predicted: float32 [3, 9, 64, 8192], P(None, None, 'theta', 'span')
- correction: float32 [9, 64, 8192], P(None, 'theta', 'span')
The draws below stay inside these ranges and needn't reach their ends.
Inputs may be any that keep to these rules, and one draw needn't show every extreme that they name: owner_map[a, r] is r // 16, or one less where r mod 16 is 0, or one more where r mod 16 is 15, never leaving the columns (r // 2048) * (128) to (r // 2048 + 1) * 128 - 1.
All inputs are finite; a program needn't handle non-finite values.
Results may differ from the reference program's by a relative error of at most 0.0001.
Values sent between devices are 32-bit elements; how exact they have to be, the bound alone decides.
A program may use at most 128 MiB of HBM per device.

```python
import math
import jax
import jax.numpy as jnp
from jax import lax

NT = 9
CA = 8
CR = 2048
BLOCKS = 8
CSWEEPS = 4
NA = 64
NR = 8192
NCA = 16
NCR = 512
N_THETA = 8
N_SPAN = 4


def draw_owner_map(key, part):
    rows = jnp.arange(NR)
    base = rows // 16
    edge = jnp.where(rows % 16 == 0, -1, jnp.where(rows % 16 == 15, 1, 0))
    moves = jax.random.randint(key, (NA, NR), 0, 2) * edge[None, :]
    low = rows // CR * (CR // 16)
    high = low + CR // 16 - 1
    return jnp.clip(base[None, :] + moves, low[None, :], high[None, :]).astype(jnp.int32)


def plant(entries, own_key, low, largest):
    shape = entries.shape
    place = [jax.random.randint(jax.random.fold_in(own_key, axis), (), 0, shape[axis]) for axis in range(len(shape))]
    entries = entries.at[tuple(place)].set(low)
    longest = shape.index(max(shape))
    place[longest] = (place[longest] + 1) % shape[longest]
    return entries.at[tuple(place)].set(largest)


def steps_of(stream_key, dims, shards, least, largest):
    gain, own = 1.0, jax.random.fold_in(stream_key, 6)
    for position, blocks in shards:
        steps = jnp.exp(jax.random.uniform(jax.random.fold_in(own, position), (blocks,), jnp.float32, least / len(shards), largest / len(shards)))
        gain = gain * jnp.repeat(steps, dims[position] // blocks).reshape([-1 if axis == position else 1 for axis in range(len(dims))])
    return gain


def noise(stream_key, extent, scale, limit, pieces=(), kind=jnp.bfloat16):
    level = steps_of(stream_key, extent, pieces, -0.22, 0.18) if pieces else 1.0
    values = jax.random.normal(stream_key, extent, jnp.float32) * scale * level
    return jnp.minimum(jnp.maximum(values, -limit), limit).astype(kind)


def setup_inputs(seed: int = 0) -> dict:
    splits = jax.random.split(jax.random.key(seed), 7)
    return {
        "velocity": noise(splits[0], (3, NT, NA, NR), 1.0, 6.0, ((2, 8), (3, 4)), jnp.float32),
        "pressure": noise(splits[1], (NT, NA, NR), 1.0, 6.0, ((1, 8), (2, 4)), jnp.float32),
        "diffusivity": jnp.clip(jnp.exp(math.log(3.0) - 2.3025851 * jax.random.uniform(splits[2], (NA, NR), jnp.float32) ** steps_of(splits[2], (NA, NR), ((0, 8), (1, 4)), -0.2, 0.2)), 0.3, 3.0),
        "live_blocks": plant(jax.random.randint(splits[3], (N_THETA, N_SPAN), 1, BLOCKS + 1), jax.random.fold_in(splits[3], 1), 1, BLOCKS).astype(jnp.int32),
        "owner_map": draw_owner_map(jax.random.fold_in(splits[6], 71), 0),
        "coarse_diag": jnp.clip(jnp.exp(math.log(4.0) - 2.0794415 * jax.random.uniform(splits[5], (NCA, NCR), jnp.float32) ** steps_of(splits[5], (NCA, NCR), ((0, 8), (1, 4)), -0.2, 0.2)), 0.5, 4.0),
    }


step_size = 0.2
viscosity = 0.5
swirl = 0.5
frequency = 0.3
relax_fine = 0.2
relax_coarse = 0.8


def spectral_matrix(count):
    rows = jnp.arange(count)[:, None]
    cols = jnp.arange(count)[None, :]
    gap = (rows - cols).astype(jnp.float32)
    parity = 1.0 - 2.0 * ((rows - cols) % 2).astype(jnp.float32)
    safe = jnp.where(rows == cols, 1.0, jnp.sin(math.pi * gap / count))
    return jnp.where(rows == cols, 0.0, frequency * 0.5 * parity / safe).astype(jnp.float32)


def grid_neighbours(field):
    zero = jnp.zeros_like(field[..., :1])
    total = jnp.roll(field, 1, -2) + jnp.roll(field, -1, -2)
    return total + jnp.concatenate([field[..., 1:], zero], -1) + jnp.concatenate([zero, field[..., :-1]], -1)


def coarse_sweeps(rhs, denom, neighbours):
    coarse = relax_coarse * rhs / denom
    for sweep in range(CSWEEPS - 1):
        applied = denom * coarse - neighbours(coarse)
        coarse = coarse + relax_coarse * (rhs - applied) / denom
    return coarse


def reference(velocity, pressure, diffusivity, live_blocks, owner_map, coarse_diag):
    spread = jnp.repeat(jnp.repeat(live_blocks, CA, 0), CR, 1)
    fluid = ((jnp.arange(NR) % CR)[None, :] < spread * (CR // BLOCKS)).astype(jnp.float32)
    coupling = spectral_matrix(NT)
    zero = jnp.zeros_like(pressure[..., :1])
    p_next_r = jnp.concatenate([pressure[..., 1:], zero], -1)
    p_prev_r = jnp.concatenate([zero, pressure[..., :-1]], -1)
    grads = [0.5 * (jnp.roll(pressure, -1, -2) - jnp.roll(pressure, 1, -2)), 0.5 * (p_next_r - p_prev_r), jnp.zeros_like(pressure)]
    parts = []
    for comp in range(3):
        field = velocity[comp]
        source = jnp.einsum('nm,mar->nar', coupling, field, precision=lax.Precision.HIGHEST)
        lap = grid_neighbours(field) - 4.0 * field
        upwind = field - jnp.roll(field, 1, -2)
        parts.append(fluid * (field + step_size * (viscosity * diffusivity * lap - swirl * upwind - source - grads[comp])))
    predicted = jnp.stack(parts, 0)
    first, second = predicted[0], predicted[1]
    zero = jnp.zeros_like(second[..., :1])
    imbalance = fluid * (0.5 * (jnp.roll(first, -1, -2) - jnp.roll(first, 1, -2)) + 0.5 * (jnp.concatenate([second[..., 1:], zero], -1) - jnp.concatenate([zero, second[..., :-1]], -1)))
    smoothed = relax_fine * imbalance
    applied = fluid * (4.0 * smoothed - grid_neighbours(smoothed)) + (1.0 - fluid) * smoothed
    remainder = imbalance - applied
    owners = ((jnp.arange(NA) // 4)[:, None] * NCR + owner_map).reshape(-1).astype(jnp.int32)
    flat = remainder.reshape(NT, -1)
    coarse_rhs = jax.vmap(lambda row: jax.ops.segment_sum(row, owners, num_segments=NCA * NCR))(flat).reshape(NT, NCA, NCR)
    coarse = coarse_sweeps(coarse_rhs, 4.0 + coarse_diag, grid_neighbours)
    lifted = coarse.reshape(NT, -1)[:, owners].reshape(NT, NA, NR)
    correction = fluid * (smoothed + lifted)
    return predicted, correction
```

```python
import functools
import math

import jax
import jax.numpy as jnp
import numpy as np
from jax import lax
from jax.experimental import pallas as pl
from jax.experimental.pallas import tpu as pltpu
from jax.sharding import PartitionSpec as P

MESH = pl.DeviceIdType.MESH
BLOCKS = 8
CSWEEPS = 4
NT = 9
FAN = 16
F32 = jnp.float32
BF16 = jnp.bfloat16

DIRS = [(1, 0), (-1, 0), (2, 0), (-2, 0)] + [
    (dt, ds) for ds in (1, -1) for dt in (0, 1, -1, 2, -2)
]
DIAG = [(1, 1), (1, -1), (-1, 1), (-1, -1)]
FREQ = [0.15 * (-1.0) ** d / math.sin(math.pi * d / NT) for d in range(1, 5)]


def kernel(
    n_theta, n_span,
    live_ref, v_ref, p_ref, d_ref, own_ref, cd_ref,
    pred_ref, corr_ref,
    tsend, trecv, ssend, srecv, dsend, drecv, bsend, brecv,
    sm_ref, stay, moved, st1, st2, edge0, lhs,
    send_sem, recv_sem,
):
    cells = v_ref.shape[1]
    cols = cells // FAN
    t, s = lax.axis_index("theta"), lax.axis_index("span")
    tile = lambda i: pl.ds(pl.multiple_of(i * 8, 8), 8)

    def peer(dt, ds):
        return (lax.rem(t + dt + n_theta, n_theta), s + ds)

    def there(ds, act):
        if ds == 0:
            act()
        elif ds > 0:
            pl.when(s < n_span - 1)(act)
        else:
            pl.when(s > 0)(act)

    def remote(src, dst, slot, dt, ds):
        return pltpu.make_async_remote_copy(
            src_ref=src, dst_ref=dst, send_sem=send_sem.at[slot], recv_sem=recv_sem.at[slot],
            device_id=peer(dt, ds), device_id_type=MESH)

    barrier = pltpu.get_barrier_semaphore()
    for dt, ds in DIRS:
        there(ds, lambda dt=dt, ds=ds: pl.semaphore_signal(
            barrier, inc=1, device_id=peer(dt, ds), device_id_type=MESH))

    lane = lax.broadcasted_iota(jnp.int32, (1, cells), 1)
    row8 = lax.broadcasted_iota(jnp.int32, (8, 1), 0)
    lane128 = lax.broadcasted_iota(jnp.int32, (8, 128), 1)
    row128 = lax.broadcasted_iota(jnp.int32, (8, 128), 0)
    live = live_ref[0, 0]
    fl = (lane < live * (cells // BLOCKS)).astype(F32)
    base = s * cols + lane // FAN
    mv = (own_ref[...] != base).astype(F32)
    df = d_ref[...] * (0.1 * fl)

    def pack(way, row, ref, plane, count):
        for i in range(count):
            tsend[way, row + i:row + i + 1, :] = ref[8 * i + plane:8 * i + plane + 1, :]

    for way, plane in ((0, 7), (1, 0)):
        pack(way, 0, v_ref, plane, 27)
        pack(way, 27, p_ref, plane, 9)
        tsend[way, 36:37, :] = df[plane:plane + 1, :]
        tsend[way, 37:38, :] = mv[plane:plane + 1, :]
        tsend[way, 38:39, :] = fl
    for i, (dt, ds) in enumerate(DIAG):
        way = 0 if dt > 0 else 1
        c0 = cells - 128 if ds > 0 else 0
        at = 127 if ds > 0 else 0
        a0 = tsend[way, 0:9, c0:c0 + 128][:, at:at + 1]
        a1 = tsend[way, 9:18, c0:c0 + 128][:, at:at + 1]
        l9 = lax.broadcasted_iota(jnp.int32, (9, 128), 1)
        dsend[i, 0:9, :] = jnp.where(l9 == 0, a0, a1)

    pl.semaphore_wait(barrier, jnp.where((s > 0) & (s < n_span - 1), 14, 9))

    m1 = [remote(tsend.at[w, 0:32], trecv.at[w, 0:32], w, 1 - 2 * w, 0) for w in range(2)]
    m2 = [remote(tsend.at[w, 32:48], trecv.at[w, 32:48], 2 + w, 1 - 2 * w, 0) for w in range(2)]
    ms = [remote(ssend.at[w], srecv.at[w], 4 + w, 0, 1 - 2 * w) for w in range(2)]
    md = [remote(dsend.at[i], drecv.at[i], 6 + i, dt, ds) for i, (dt, ds) in enumerate(DIAG)]
    mb = [remote(bsend, brecv.at[i], 10 + i, dt, ds) for i, (dt, ds) in enumerate(DIRS)]
    for m in m1:
        m.start()
    for m, (dt, ds) in zip(md, DIAG):
        there(ds, m.start)

    def clear(ds):
        w = 0 if ds < 0 else 1
        srecv[w] = jnp.zeros(srecv.shape[1:], F32)
        for i, (_, e) in enumerate(DIAG):
            if e == -ds:
                drecv[i] = jnp.zeros(drecv.shape[1:], F32)
        for i, (_, e) in enumerate(DIRS):
            if e == -ds:
                brecv[i] = jnp.zeros(brecv.shape[1:], F32)

    pl.when(s == 0)(lambda: clear(-1))
    pl.when(s == n_span - 1)(lambda: clear(1))

    def a_pair(x):
        return (jnp.where(row8 == 7, 0.0, pltpu.roll(x, 7, 0)),
                jnp.where(row8 == 0, 0.0, pltpu.roll(x, 1, 0)))

    def r_pair(x):
        return (jnp.where(lane == cells - 1, 0.0, pltpu.roll(x, cells - 1, 1)),
                jnp.where(lane == 0, 0.0, pltpu.roll(x, 1, 1)))

    width = 256
    for c in range(3):
        def source(j, _):
            at = pl.ds(pl.multiple_of(j * width, width), width)
            x = [v_ref[(c * NT + n) * 8:(c * NT + n) * 8 + 8, at] for n in range(NT)]
            acc = list(x)
            for d in range(1, 5):
                for n in range(NT):
                    gap = (x[(n - d) % NT] - x[(n + d) % NT]) * (0.2 * FREQ[d - 1])
                    acc[n] = acc[n] - gap
            for n in range(NT):
                pred_ref[(c * NT + n) * 8:(c * NT + n) * 8 + 8, at] = acc[n]
            return 0

        lax.fori_loop(0, cells // width, source, 0)

        def local(n, _):
            x = v_ref[tile(c * NT + n), :]
            ap, am = a_pair(x)
            rp, rm = r_pair(x)
            out = pred_ref[tile(c * NT + n), :] - 0.1 * (x - am)
            if c < 2:
                q = p_ref[tile(n), :]
                qp, qm = a_pair(q) if c == 0 else r_pair(q)
                out = out - 0.1 * (qp - qm)
            pred_ref[tile(c * NT + n), :] = fl * out + df * (ap + am + rp + rm - 4.0 * x)
            return 0

        lax.fori_loop(0, NT, local, 0)

        if c == 0:
            for way, plane in ((0, 7), (1, 0)):
                pack(way, 39, pred_ref, plane, 9)
                m2[way].start()
        if c == 1:
            def columns(n, _):
                for way in range(2):
                    c0, at = (cells - 128, 127) if way == 0 else (0, 0)
                    got = jnp.zeros((8, 128), F32)
                    for f, x in enumerate((
                        v_ref[tile(n), c0:c0 + 128], v_ref[tile(NT + n), c0:c0 + 128],
                        v_ref[tile(2 * NT + n), c0:c0 + 128], p_ref[tile(n), c0:c0 + 128],
                        pred_ref[tile(NT + n), c0:c0 + 128], df[:, c0:c0 + 128],
                        jnp.broadcast_to(fl[:, c0:c0 + 128], (8, 128)))):
                        got = jnp.where(lane128 == f, x[:, at:at + 1], got)
                    ssend[way, tile(n), :] = got
                return 0

            lax.fori_loop(0, NT, columns, 0)
            for m, ds in zip(ms, (1, -1)):
                there(ds, m.start)

    def members(j, _):
        at = pl.ds(pl.multiple_of(j * width, width), width)
        r = lax.broadcasted_iota(jnp.int32, (256, width), 1) + j * width
        k = lax.broadcasted_iota(jnp.int32, (256, width), 0) & 127
        b = r // FAN
        e = r % FAN
        to = jnp.where(e == 0, b - 1, jnp.where(e == FAN - 1, b + 1, -9))
        st1[:, at] = (b == k).astype(F32).astype(BF16)
        st2[:, at] = (to == k).astype(F32).astype(BF16)
        return 0

    lax.fori_loop(0, cells // width, members, 0)

    for m in m1 + m2:
        m.wait_recv()
    for m, (dt, ds) in zip(md, DIAG):
        there(-ds, m.wait_recv)
    for m, ds in zip(ms, (1, -1)):
        there(-ds, m.wait_recv)

    df_dn, fl_dn = trecv[0, 36:37, :], trecv[0, 38:39, :]
    df_up, fl_up = trecv[1, 36:37, :], trecv[1, 38:39, :]
    lo, hi = lane == 0, lane == cells - 1
    edge0[0] = (trecv[0, 39:48, :] + df_dn * tsend[1, 0:9, :] - 0.1 * fl_dn * tsend[1, 27:36, :]
                + jnp.where(lo, df_dn * drecv[0, 0:9, 0:1], 0.0)
                + jnp.where(hi, df_dn * drecv[1, 0:9, 0:1], 0.0))
    edge0[1] = (trecv[1, 39:48, :] + (df_up + 0.1 * fl_up) * tsend[0, 0:9, :]
                + 0.1 * fl_up * tsend[0, 27:36, :]
                + jnp.where(lo, df_up * drecv[2, 0:9, 0:1], 0.0)
                + jnp.where(hi, df_up * drecv[3, 0:9, 0:1], 0.0))
    w_dn = jnp.where(row8 == 0, df + 0.1 * fl, 0.0)
    w_up = jnp.where(row8 == 7, df, 0.0)
    q_dn = jnp.where(row8 == 0, 0.1 * fl, 0.0)
    q_up = jnp.where(row8 == 7, 0.1 * fl, 0.0)

    def complete(n, _):
        left, right = srecv[0, tile(n), :], srecv[1, tile(n), :]
        for c in range(3):
            i = c * NT + n
            out = (pred_ref[tile(i), :] + w_dn * trecv[0, pl.ds(i, 1), :]
                   + w_up * trecv[1, pl.ds(i, 1), :])
            a, b = df * left[:, c:c + 1], df * right[:, c:c + 1]
            if c == 0:
                out = (out + q_dn * trecv[0, pl.ds(27 + n, 1), :]
                       - q_up * trecv[1, pl.ds(27 + n, 1), :])
            if c == 1:
                a = a + 0.1 * fl * left[:, 3:4]
                b = b - 0.1 * fl * right[:, 3:4]
            out = out + jnp.where(lo, a, 0.0) + jnp.where(hi, b, 0.0)
            pred_ref[tile(i), :] = out
        first, second = pred_ref[tile(n), :], pred_ref[tile(NT + n), :]
        fp = jnp.where(row8 == 7, edge0[1, pl.ds(n, 1), :], pltpu.roll(first, 7, 0))
        fm = jnp.where(row8 == 0, edge0[0, pl.ds(n, 1), :], pltpu.roll(first, 1, 0))
        x = [v_ref[tile(NT + n), 0:128][:, 0:1],
             v_ref[tile(NT + n), cells - 128:cells][:, 127:128]]
        q = [p_ref[tile(n), 0:128][:, 0:1], p_ref[tile(n), cells - 128:cells][:, 127:128]]
        rows = pl.ds(n, 1)

        def corner(side, dn, up):
            return (jnp.where(row8 == 0, (side[:, 5:6] + 0.1 * side[:, 6:7]) * drecv[dn, rows, :][:, 1:2], 0.0)
                    + jnp.where(row8 == 7, side[:, 5:6] * drecv[up, rows, :][:, 1:2], 0.0))

        pl1 = (left[:, 4:5] + left[:, 5:6] * x[0] - 0.1 * left[:, 6:7] * q[0]
               + corner(left, 0, 2))
        pr1 = (right[:, 4:5] + right[:, 5:6] * x[1] + 0.1 * right[:, 6:7] * q[1]
               + corner(right, 1, 3))
        sp = jnp.where(hi, pr1, pltpu.roll(second, cells - 1, 1))
        sn = jnp.where(lo, pl1, pltpu.roll(second, 1, 1))
        sm = 0.1 * fl * (fp - fm + sp - sn)
        sm_ref[tile(n), :] = sm
        ap, am = a_pair(sm)
        rp, rm = r_pair(sm)
        rem = fl * (sm + (ap + am + rp + rm))
        gone = rem * mv
        kept = rem - gone
        at = pl.ds(pl.multiple_of(n * 16, 16), 16)
        for ref, x in ((stay, kept), (moved, gone)):
            top = x.astype(BF16).astype(F32)
            ref[at, :] = jnp.concatenate([top, x - top], 0).astype(BF16)
        e = jnp.where(lane128 == 0, sm[:, cells - 1:cells],
                      jnp.where(lane128 == 127, sm[:, 0:1] * left[:, 6:7], 0.0))
        e0 = jnp.sum(e[0:4], axis=0, keepdims=True)
        e1 = jnp.sum(e[4:8], axis=0, keepdims=True)
        bsend[tile(n), :] = jnp.where(row128 == 5, e0, jnp.where(row128 == 6, e1, 0.0))
        return 0

    lax.fori_loop(0, NT, complete, 0)

    def pieces(x):
        top = x.astype(BF16).astype(F32)
        return [top, x - top]

    zero7 = jnp.zeros((7, cells), F32)
    kept, gone = [], []
    for w, plane in ((0, 0), (1, 7)):
        x = jnp.concatenate([sm_ref[8 * i + plane:8 * i + plane + 1, :] for i in range(NT)], 0)
        x = x * trecv[w, 38:39, :]
        g = x * trecv[w, 37:38, :]
        for rows, y in ((kept, x - g), (gone, g)):
            for z in pieces(y):
                rows += [z, zero7]
    for ref, rows in ((stay, kept), (moved, gone)):
        for i in range(4):
            at = 16 * NT + 16 * i
            ref[at:at + 16, :] = jnp.concatenate(rows[2 * i:2 * i + 2], 0).astype(BF16)

    nt = (((1,), (1,)), ((), ()))
    tot = (lax.dot_general(stay[...], st1[0:128, :], nt, preferred_element_type=F32)
           + lax.dot_general(moved[...], st2[0:128, :], nt, preferred_element_type=F32))
    e_dn = tot[16 * NT:16 * NT + 16] + tot[16 * NT + 16:16 * NT + 32]
    e_up = tot[16 * NT + 32:16 * NT + 48] + tot[16 * NT + 48:16 * NT + 64]
    for n in range(NT):
        x = tot[16 * n:16 * n + 8] + tot[16 * n + 8:16 * n + 16]
        x0 = jnp.sum(x[0:4], axis=0, keepdims=True)
        x1 = jnp.sum(x[4:8], axis=0, keepdims=True)
        old = bsend[n * 8:n * 8 + 8, :]
        bsend[n * 8:n * 8 + 8, :] = jnp.where(
            row128 == 0, e_dn[n:n + 1], jnp.where(row128 == 1, x0, jnp.where(
                row128 == 2, x1, jnp.where(row128 == 3, e_up[n:n + 1], old))))
    bsend[72:74, :] = cd_ref[...]
    bsend[74:80, :] = jnp.zeros((6, 128), F32)
    for m, (dt, ds) in zip(mb, DIRS):
        there(ds, m.start)
    for m, (dt, ds) in zip(mb, DIRS):
        there(-ds, m.wait_recv)

    def keep(x, rows):
        return jnp.where((row128 >= rows[0]) & (row128 < rows[1]), x, 0.0)

    left_half = lane128 >= 64
    d0, d1 = jnp.zeros((8, 128), F32), jnp.zeros((8, 128), F32)
    for i, (dt, ds) in [(None, (0, 0))] + list(enumerate(DIRS)):
        x = bsend[72:80, :] if i is None else brecv[i, 72:80, :]
        ot, os = -dt, -ds
        x = keep(x, (1, 2) if ot == -2 else (0, 1) if ot == 2 else (0, 2))
        x = pltpu.roll(x, (3 + 2 * ot) % 8, 0)
        if os == 0:
            d0 = d0 + x
        else:
            d1 = d1 + jnp.where(left_half == (os < 0), x, 0.0)
    ok = jnp.where(left_half, (s > 0).astype(F32), (s < n_span - 1).astype(F32))
    inv = jnp.concatenate([0.8 / (4.0 + d0), ok * 0.8 / (4.0 + d1)], 1)

    def coarse(n, _):
        r0, r1 = jnp.zeros((8, 128), F32), jnp.zeros((8, 128), F32)
        for i, (dt, ds) in [(None, (0, 0))] + list(enumerate(DIRS)):
            x = bsend[tile(n), :] if i is None else brecv[i, tile(n), :]
            ot, os = -dt, -ds
            rows = (2, 4) if ot == -2 else (0, 2) if ot == 2 else (0, 4)
            sh = (2 * ot + 2) % 8
            main = pltpu.roll(keep(x, rows), sh, 0) if sh else keep(x, rows)
            side = pltpu.roll(keep(x, (rows[0] + 4, rows[1] + 4)), (sh + 4) % 8, 0) if (sh + 4) % 8 else keep(x, (rows[0] + 4, rows[1] + 4))
            if os == 0:
                r0, r1 = r0 + main, r1 + side
            else:
                r1 = r1 + jnp.where(left_half == (os < 0), main, 0.0)
                r0 = r0 + jnp.where(lane128 == (0 if os < 0 else 127), side, 0.0)
        rhs = jnp.concatenate([r0, r1], 1)
        x = inv * rhs
        for _ in range(CSWEEPS - 1):
            around = (pltpu.roll(x, 1, 0) + pltpu.roll(x, 7, 0)
                      + pltpu.roll(x, 1, 1) + pltpu.roll(x, 255, 1))
            x = 0.2 * x + inv * (rhs + around)
        mine = jnp.where(row128 < 4, x[3:4, 0:128], x[4:5, 0:128])
        top = mine.astype(BF16).astype(F32)
        lhs[tile(n), :] = jnp.concatenate([top, mine - top], 1)
        return 0

    lax.fori_loop(0, NT, coarse, 0)

    def lift(j, _):
        at = pl.ds(pl.multiple_of(j * width, width), width)
        x = lhs[...].astype(BF16)
        l1 = jnp.dot(x, st1[:, at], preferred_element_type=F32)
        l2 = jnp.dot(x, st2[:, at], preferred_element_type=F32)
        r = lax.broadcasted_iota(jnp.int32, (8, width), 1) + j * width
        f = (r < live * (cells // BLOCKS)).astype(F32)
        away = own_ref[:, at] != s * cols + r // FAN
        for n in range(NT):
            k = slice(n * 8, n * 8 + 8)
            corr_ref[k, at] = f * (sm_ref[k, at] + jnp.where(away, l2[k], l1[k]))
        return 0

    lax.fori_loop(0, cells // width, lift, 0)

    for m in m1 + m2:
        m.wait_send()
    for m, ds in list(zip(ms, (1, -1))) + [(m, d[1]) for m, d in zip(md, DIAG)] + [
            (m, d[1]) for m, d in zip(mb, DIRS)]:
        there(ds, m.wait_send)


def shards(n_theta, n_span, velocity, pressure, diffusivity, live_blocks, owner_map, coarse_diag):
    ncomp, ntime, planes, cells = velocity.shape
    vmem = pl.BlockSpec(memory_space=pltpu.VMEM)
    n = len(DIRS)
    pred, corr = pl.pallas_call(
        functools.partial(kernel, n_theta, n_span),
        out_shape=(
            jax.ShapeDtypeStruct((ncomp * ntime * planes, cells), F32),
            jax.ShapeDtypeStruct((ntime * planes, cells), F32),
        ),
        in_specs=[pl.BlockSpec(memory_space=pltpu.SMEM)] + [vmem] * 5,
        out_specs=(vmem, vmem),
        scratch_shapes=[
            pltpu.VMEM((2, 48, cells), F32),
            pltpu.VMEM((2, 48, cells), F32),
            pltpu.VMEM((2, 72, 128), F32),
            pltpu.VMEM((2, 72, 128), F32),
            pltpu.VMEM((4, 16, 128), F32),
            pltpu.VMEM((4, 16, 128), F32),
            pltpu.VMEM((80, 128), F32),
            pltpu.VMEM((n, 80, 128), F32),
            pltpu.VMEM((72, cells), F32),
            pltpu.VMEM((208, cells), BF16),
            pltpu.VMEM((208, cells), BF16),
            pltpu.VMEM((256, cells), BF16),
            pltpu.VMEM((256, cells), BF16),
            pltpu.VMEM((2, 9, cells), F32),
            pltpu.VMEM((72, 256), F32),
            pltpu.SemaphoreType.DMA((10 + n,)),
            pltpu.SemaphoreType.DMA((10 + n,)),
        ],
        compiler_params=pltpu.CompilerParams(
            collective_id=0, has_side_effects=True, vmem_limit_bytes=48 * 2**20),
    )(
        live_blocks,
        velocity.reshape(ncomp * ntime * planes, cells),
        pressure.reshape(ntime * planes, cells),
        diffusivity, owner_map, coarse_diag,
    )
    return pred.reshape(velocity.shape), corr.reshape(pressure.shape)


def solution(mesh):
    return jax.shard_map(
        functools.partial(shards, mesh.shape["theta"], mesh.shape["span"]),
        mesh=mesh,
        in_specs=(
            P(None, None, "theta", "span"),
            P(None, "theta", "span"),
            P("theta", "span"),
            P("theta", "span"),
            P("theta", "span"),
            P("theta", "span"),
        ),
        out_specs=(P(None, None, "theta", "span"), P(None, "theta", "span")),
        check_vma=False,
    )
```

```python
import functools
import math

import jax
import jax.numpy as jnp
import numpy as np
from jax import lax
from jax.experimental import pallas as pl
from jax.experimental.pallas import tpu as pltpu
from jax.sharding import PartitionSpec as P

MESH = pl.DeviceIdType.MESH
BLOCKS = 8
CSWEEPS = 4
NT = 9
FAN = 16
F32 = jnp.float32
BF16 = jnp.bfloat16

DIRS = [(1, 0), (-1, 0), (2, 0), (-2, 0)] + [
    (dt, ds) for ds in (1, -1) for dt in (0, 1, -1, 2, -2)
]
DIAG = [(1, 1), (1, -1), (-1, 1), (-1, -1)]
FREQ = [0.15 * (-1.0) ** d / math.sin(math.pi * d / NT) for d in range(1, 5)]


def kernel(
    n_theta, n_span,
    live_ref, v_hbm, p_hbm, d_hbm, own_hbm, cd_hbm,
    pred_ref, sm_ref, lhs,
    v_ref, p_ref, d_ref, own_ref, cd_ref,
    tsend, trecv, ssend, srecv, dsend, drecv, bsend, brecv,
    psend, precv, side_ref, stay, moved, st1, st2, edge0,
    send_sem, recv_sem, load_sem,
):
    cells = v_ref.shape[1]
    cols = cells // FAN
    t, s = lax.axis_index("theta"), lax.axis_index("span")
    third = NT * 8
    loads = [pltpu.make_async_copy(v_hbm.at[third * c:third * c + third], v_ref.at[third * c:third * c + third],
                                   load_sem.at[c]) for c in range(3)]
    loads += [pltpu.make_async_copy(a, b, load_sem.at[3 + i]) for i, (a, b) in enumerate((
        (p_hbm, p_ref), (d_hbm, d_ref), (own_hbm, own_ref), (cd_hbm, cd_ref)))]
    for m in loads:
        m.start()
    tile = lambda i: pl.ds(pl.multiple_of(i * 8, 8), 8)

    def peer(dt, ds):
        return (lax.rem(t + dt + n_theta, n_theta), s + ds)

    def there(ds, act):
        if ds == 0:
            act()
        elif ds > 0:
            pl.when(s < n_span - 1)(act)
        else:
            pl.when(s > 0)(act)

    def remote(src, dst, slot, dt, ds):
        return pltpu.make_async_remote_copy(
            src_ref=src, dst_ref=dst, send_sem=send_sem.at[slot], recv_sem=recv_sem.at[slot],
            device_id=peer(dt, ds), device_id_type=MESH)

    barrier = pltpu.get_barrier_semaphore()
    for dt, ds in DIRS:
        there(ds, lambda dt=dt, ds=ds: pl.semaphore_signal(
            barrier, inc=1, device_id=peer(dt, ds), device_id_type=MESH))

    lane = lax.broadcasted_iota(jnp.int32, (1, cells), 1)
    row8 = lax.broadcasted_iota(jnp.int32, (8, 1), 0)
    lane128 = lax.broadcasted_iota(jnp.int32, (8, 128), 1)
    row128 = lax.broadcasted_iota(jnp.int32, (8, 128), 0)
    for m in loads:
        m.wait()
    fl = (lane < live_ref[0, 0] * (cells // BLOCKS)).astype(F32)
    base = s * cols + (lane >> 4)
    mv = (own_ref[...] != base).astype(F32)
    df = d_ref[...] * (0.1 * fl)

    def pack(way, row, ref, plane, count):
        for i in range(count):
            tsend[way, row + i:row + i + 1, :] = ref[8 * i + plane:8 * i + plane + 1, :]

    for way, plane in ((0, 7), (1, 0)):
        pack(way, 0, v_ref, plane, 27)
        pack(way, 27, p_ref, plane, 9)
        tsend[way, 36:37, :] = df[plane:plane + 1, :]
        tsend[way, 37:38, :] = mv[plane:plane + 1, :]
        tsend[way, 38:39, :] = fl
    for i, (dt, ds) in enumerate(DIAG):
        way = 0 if dt > 0 else 1
        c0 = cells - 128 if ds > 0 else 0
        at = 127 if ds > 0 else 0
        a0 = tsend[way, 0:9, c0:c0 + 128][:, at:at + 1]
        a1 = tsend[way, 9:18, c0:c0 + 128][:, at:at + 1]
        l9 = lax.broadcasted_iota(jnp.int32, (9, 128), 1)
        dsend[i, 0:9, :] = jnp.where(l9 == 0, a0, a1)

    pl.semaphore_wait(barrier, jnp.where((s > 0) & (s < n_span - 1), 14, 9))

    m1 = [remote(tsend.at[w, 0:32], trecv.at[w, 0:32], w, 1 - 2 * w, 0) for w in range(2)]
    m2 = [remote(tsend.at[w, 32:48], trecv.at[w, 32:48], 2 + w, 1 - 2 * w, 0) for w in range(2)]
    ms = [remote(ssend.at[w], srecv.at[w], 4 + w, 0, 1 - 2 * w) for w in range(2)]
    md = [remote(dsend.at[i], drecv.at[i], 6 + i, dt, ds) for i, (dt, ds) in enumerate(DIAG)]
    mb = [remote(bsend, brecv.at[i], 10 + i, dt, ds) if ds == 0 else
          remote(psend.at[(1 - ds) // 2], precv.at[i - 4], 10 + i, dt, ds)
          for i, (dt, ds) in enumerate(DIRS)]
    for m in m1:
        m.start()
    for m, (dt, ds) in zip(md, DIAG):
        there(ds, m.start)

    def clear(ds):
        w = 0 if ds < 0 else 1
        srecv[w] = jnp.zeros(srecv.shape[1:], F32)
        for i, (_, e) in enumerate(DIAG):
            if e == -ds:
                drecv[i] = jnp.zeros(drecv.shape[1:], F32)
        for i, (_, e) in enumerate(DIRS):
            if e == -ds:
                precv[i - 4] = jnp.zeros(precv.shape[1:], F32)

    pl.when(s == 0)(lambda: clear(-1))
    pl.when(s == n_span - 1)(lambda: clear(1))

    def a_pair(x):
        return (jnp.where(row8 == 7, 0.0, pltpu.roll(x, 7, 0)),
                jnp.where(row8 == 0, 0.0, pltpu.roll(x, 1, 0)))

    def r_pair(x):
        return (jnp.where(lane == cells - 1, 0.0, pltpu.roll(x, cells - 1, 1)),
                jnp.where(lane == 0, 0.0, pltpu.roll(x, 1, 1)))

    width = 256
    for c in range(3):
        def source(j, _):
            at = pl.ds(pl.multiple_of(j * width, width), width)
            x = [v_ref[(c * NT + n) * 8:(c * NT + n) * 8 + 8, at] for n in range(NT)]
            acc = list(x)
            for d in range(1, 5):
                for n in range(NT):
                    gap = (x[(n - d) % NT] - x[(n + d) % NT]) * (0.2 * FREQ[d - 1])
                    acc[n] = acc[n] - gap
            for n in range(NT):
                pred_ref[(c * NT + n) * 8:(c * NT + n) * 8 + 8, at] = acc[n]
            return 0

        lax.fori_loop(0, cells // width, source, 0)

        def local(n, _):
            x = v_ref[tile(c * NT + n), :]
            ap, am = a_pair(x)
            rp, rm = r_pair(x)
            out = pred_ref[tile(c * NT + n), :] - 0.1 * (x - am)
            if c < 2:
                q = p_ref[tile(n), :]
                qp, qm = a_pair(q) if c == 0 else r_pair(q)
                out = out - 0.1 * (qp - qm)
            pred_ref[tile(c * NT + n), :] = fl * out + df * (ap + am + rp + rm - 4.0 * x)
            return 0

        lax.fori_loop(0, NT, local, 0)

        if c == 0:
            for way, plane in ((0, 7), (1, 0)):
                pack(way, 39, pred_ref, plane, 9)
                m2[way].start()
        if c == 1:
            def columns(n, _):
                for way in range(2):
                    c0, at = (cells - 128, 127) if way == 0 else (0, 0)
                    got = jnp.zeros((8, 128), F32)
                    for f, x in enumerate((
                        v_ref[tile(n), c0:c0 + 128], v_ref[tile(NT + n), c0:c0 + 128],
                        v_ref[tile(2 * NT + n), c0:c0 + 128], p_ref[tile(n), c0:c0 + 128],
                        pred_ref[tile(NT + n), c0:c0 + 128], df[:, c0:c0 + 128],
                        jnp.broadcast_to(fl[:, c0:c0 + 128], (8, 128)))):
                        got = jnp.where(lane128 == f, x[:, at:at + 1], got)
                    ssend[way, tile(n), :] = got
                return 0

            lax.fori_loop(0, NT, columns, 0)
            for m, ds in zip(ms, (1, -1)):
                there(ds, m.start)

    def members(j, _):
        at = pl.ds(pl.multiple_of(j * width, width), width)
        r = lax.broadcasted_iota(jnp.int32, (128, width), 1) + j * width
        k = lax.broadcasted_iota(jnp.int32, (128, width), 0)
        b = r >> 4
        e = r & (FAN - 1)
        to = jnp.where(e == 0, b - 1, jnp.where(e == FAN - 1, b + 1, -9))
        st1[:, at] = (b == k).astype(F32).astype(BF16)
        st2[:, at] = (to == k).astype(F32).astype(BF16)
        return 0

    lax.fori_loop(0, cells // width, members, 0)

    for m in m1 + m2:
        m.wait_recv()
    for m, (dt, ds) in zip(md, DIAG):
        there(-ds, m.wait_recv)
    for m, ds in zip(ms, (1, -1)):
        there(-ds, m.wait_recv)

    df_dn, fl_dn = trecv[0, 36:37, :], trecv[0, 38:39, :]
    df_up, fl_up = trecv[1, 36:37, :], trecv[1, 38:39, :]
    lo, hi = lane == 0, lane == cells - 1
    edge0[0] = (trecv[0, 39:48, :] + df_dn * tsend[1, 0:9, :] - 0.1 * fl_dn * tsend[1, 27:36, :]
                + jnp.where(lo, df_dn * drecv[0, 0:9, 0:1], 0.0)
                + jnp.where(hi, df_dn * drecv[1, 0:9, 0:1], 0.0))
    edge0[1] = (trecv[1, 39:48, :] + (df_up + 0.1 * fl_up) * tsend[0, 0:9, :]
                + 0.1 * fl_up * tsend[0, 27:36, :]
                + jnp.where(lo, df_up * drecv[2, 0:9, 0:1], 0.0)
                + jnp.where(hi, df_up * drecv[3, 0:9, 0:1], 0.0))
    w_dn = jnp.where(row8 == 0, df + 0.1 * fl, 0.0)
    w_up = jnp.where(row8 == 7, df, 0.0)
    q_dn = jnp.where(row8 == 0, 0.1 * fl, 0.0)
    q_up = jnp.where(row8 == 7, 0.1 * fl, 0.0)

    def complete(n, _):
        left, right = srecv[0, tile(n), :], srecv[1, tile(n), :]
        for c in range(3):
            i = c * NT + n
            out = (pred_ref[tile(i), :] + w_dn * trecv[0, pl.ds(i, 1), :]
                   + w_up * trecv[1, pl.ds(i, 1), :])
            if c == 0:
                out = (out + q_dn * trecv[0, pl.ds(27 + n, 1), :]
                       - q_up * trecv[1, pl.ds(27 + n, 1), :])
            pred_ref[tile(i), :] = out
            for c0, col, side, sign in ((0, 0, left, 0.1), (cells - 128, 127, right, -0.1)):
                at = slice(c0, c0 + 128)
                x = df[:, at] * side[:, c:c + 1]
                if c == 1:
                    x = x + sign * fl[:, at] * side[:, 3:4]
                pred_ref[tile(i), at] += jnp.where(lane128 == col, x, 0.0)
        first, second = pred_ref[tile(n), :], pred_ref[tile(NT + n), :]
        fp = jnp.where(row8 == 7, edge0[1, pl.ds(n, 1), :], pltpu.roll(first, 7, 0))
        fm = jnp.where(row8 == 0, edge0[0, pl.ds(n, 1), :], pltpu.roll(first, 1, 0))
        x = [v_ref[tile(NT + n), 0:128][:, 0:1],
             v_ref[tile(NT + n), cells - 128:cells][:, 127:128]]
        q = [p_ref[tile(n), 0:128][:, 0:1], p_ref[tile(n), cells - 128:cells][:, 127:128]]
        rows = pl.ds(n, 1)

        def corner(side, dn, up):
            return (jnp.where(row8 == 0, (side[:, 5:6] + 0.1 * side[:, 6:7]) * drecv[dn, rows, :][:, 1:2], 0.0)
                    + jnp.where(row8 == 7, side[:, 5:6] * drecv[up, rows, :][:, 1:2], 0.0))

        pl1 = (left[:, 4:5] + left[:, 5:6] * x[0] - 0.1 * left[:, 6:7] * q[0]
               + corner(left, 0, 2))
        pr1 = (right[:, 4:5] + right[:, 5:6] * x[1] + 0.1 * right[:, 6:7] * q[1]
               + corner(right, 1, 3))
        sp = jnp.where(hi, pr1, pltpu.roll(second, cells - 1, 1))
        sn = jnp.where(lo, pl1, pltpu.roll(second, 1, 1))
        sm = 0.1 * fl * (fp - fm + sp - sn)
        sm_ref[tile(n), :] = sm
        ap, am = a_pair(sm)
        rp, rm = r_pair(sm)
        rem = fl * (sm + (ap + am + rp + rm))
        gone = rem * mv
        kept = rem - gone
        at = pl.ds(pl.multiple_of(n * 16, 16), 16)
        for ref, x in ((stay, kept), (moved, gone)):
            top = x.astype(BF16).astype(F32)
            ref[at, :] = jnp.concatenate([top, x - top], 0).astype(BF16)
        e = jnp.where(lane128 == 0, sm[:, cells - 1:cells],
                      jnp.where(lane128 == 127, sm[:, 0:1] * left[:, 6:7], 0.0))
        e0 = jnp.sum(e[0:4], axis=0, keepdims=True)
        e1 = jnp.sum(e[4:8], axis=0, keepdims=True)
        side_ref[tile(n), :] = jnp.where(row128 == 5, e0, jnp.where(row128 == 6, e1, 0.0))
        return 0

    lax.fori_loop(0, NT, complete, 0)

    def pieces(x):
        top = x.astype(BF16).astype(F32)
        return [top, x - top]

    zero7 = jnp.zeros((7, cells), F32)
    kept, gone = [], []
    for w, plane in ((0, 0), (1, 7)):
        x = jnp.concatenate([sm_ref[8 * i + plane:8 * i + plane + 1, :] for i in range(NT)], 0)
        x = x * trecv[w, 38:39, :]
        g = x * trecv[w, 37:38, :]
        for rows, y in ((kept, x - g), (gone, g)):
            for z in pieces(y):
                rows += [z, zero7]
    for ref, rows in ((stay, kept), (moved, gone)):
        for i in range(4):
            at = 16 * NT + 16 * i
            ref[at:at + 16, :] = jnp.concatenate(rows[2 * i:2 * i + 2], 0).astype(BF16)

    nt = (((1,), (1,)), ((), ()))
    tot = (lax.dot_general(stay[...], st1[...], nt, preferred_element_type=F32)
           + lax.dot_general(moved[...], st2[...], nt, preferred_element_type=F32))
    e_dn = tot[16 * NT:16 * NT + 16] + tot[16 * NT + 16:16 * NT + 32]
    e_up = tot[16 * NT + 32:16 * NT + 48] + tot[16 * NT + 48:16 * NT + 64]
    pack_r, pack_l = jnp.zeros((8, 128), F32), jnp.zeros((8, 128), F32)
    main, sides = [], jnp.zeros((8, 128), F32)
    for n in range(NT):
        x = tot[16 * n:16 * n + 8] + tot[16 * n + 8:16 * n + 16]
        x0 = jnp.sum(x[0:4], axis=0, keepdims=True)
        x1 = jnp.sum(x[4:8], axis=0, keepdims=True)
        x = jnp.where(row128 == 0, e_dn[n:n + 1], jnp.where(row128 == 1, x0, jnp.where(
            row128 == 2, x1, jnp.where(row128 == 3, e_up[n:n + 1], side_ref[n * 8:n * 8 + 8, :]))))
        main.append(x)
        slot = (lane128 >> 2) == n
        pack_r = jnp.where(slot, pltpu.roll(x, 3 + 4 * n, 1), pack_r)
        pack_l = jnp.where(slot, pltpu.roll(x, 1 + 4 * n, 1), pack_l)
        sides = jnp.where((lane128 >> 1) == n, pltpu.roll(x, 1 + 2 * n, 1), sides)
    cd = jnp.concatenate([cd_ref[...], jnp.zeros((6, 128), F32)], 0)
    for i in range(5):
        y = main[2 * i + 1] if 2 * i + 1 < NT else jnp.zeros((8, 128), F32)
        bsend[8 * i:8 * i + 8, :] = jnp.where(row128 < 4, main[2 * i], pltpu.roll(y, 4, 0))
    bsend[40:48, :] = jnp.where(row128 < 4, cd, sides)
    cslot = (lane128 >> 2) == 10
    psend[0] = jnp.where(cslot, pltpu.roll(cd, 43, 1), pack_r)
    psend[1] = jnp.where(cslot, pltpu.roll(cd, 41, 1), pack_l)
    for m, (dt, ds) in zip(mb, DIRS):
        there(ds, m.start)
    for m, (dt, ds) in zip(mb, DIRS):
        there(-ds, m.wait_recv)

    def keep(x, rows):
        return jnp.where((row128 >= rows[0]) & (row128 < rows[1]), x, 0.0)

    def turn(x, by, axis):
        return pltpu.roll(x, by % x.shape[axis], axis) if by % x.shape[axis] else x

    def rows_of(ot):
        return (2, 4) if ot == -2 else (0, 2) if ot == 2 else (0, 4)

    def diag_rows(x, ot):
        return turn(keep(x, (1, 2) if ot == -2 else (0, 1) if ot == 2 else (0, 2)), 3 + 2 * ot, 0)

    near = [(0, bsend)] + [(-dt, brecv.at[i]) for i, (dt, ds) in enumerate(DIRS) if ds == 0]
    d0 = sum(diag_rows(ref[40:48, :], ot) for ot, ref in near)
    beside = []
    for sent in (1, -1):
        got = [(-dt, precv[i - 4]) for i, (dt, ds) in enumerate(DIRS) if ds == sent]
        beside.append((
            sum(turn(keep(x, rows_of(ot)), 2 * ot + 2, 0) for ot, x in got),
            sum(turn(keep(x, (rows_of(ot)[0] + 4, rows_of(ot)[1] + 4)), 2 * ot + 6, 0) for ot, x in got),
            sum(diag_rows(x, ot) for ot, x in got)))
    s_near = sum(turn(keep(ref[40:48, :], (rows_of(ot)[0] + 4, rows_of(ot)[1] + 4)), 2 * ot + 6, 0)
                 for ot, ref in near)
    (ml, sl, dl), (mr, sr, dr) = beside
    from_left, from_right = lane128 >= 125, lane128 <= 2
    d1 = (jnp.where(from_left, turn(dl, -43, 1), 0.0) + jnp.where(from_right, turn(dr, -41, 1), 0.0))
    ok = jnp.where(lane128 >= 64, (s > 0).astype(F32), (s < n_span - 1).astype(F32))
    inv = jnp.concatenate([0.8 / (4.0 + d0), ok * 0.8 / (4.0 + d1)], 1)
    for n in range(NT):
        lo4 = 4 * (n % 2)
        r0 = sum(turn(keep(ref[8 * (n // 2):8 * (n // 2) + 8, :], (rows_of(ot)[0] + lo4, rows_of(ot)[1] + lo4)),
                      2 * ot + 2 - lo4, 0) for ot, ref in near)
        r0 = r0 + jnp.where(lane128 == 0, turn(sl, -(3 + 4 * n), 1), 0.0)
        r0 = r0 + jnp.where(lane128 == 127, turn(sr, -(1 + 4 * n), 1), 0.0)
        r1 = jnp.where((lane128 == 0) | (lane128 == 127), turn(s_near, -(1 + 2 * n), 1), 0.0)
        r1 = r1 + jnp.where(from_left, turn(ml, -(3 + 4 * n), 1), 0.0)
        r1 = r1 + jnp.where(from_right, turn(mr, -(1 + 4 * n), 1), 0.0)
        rhs = jnp.concatenate([r0, r1], 1)
        x = inv * rhs
        for _ in range(CSWEEPS - 1):
            around = (pltpu.roll(x, 1, 0) + pltpu.roll(x, 7, 0)
                      + pltpu.roll(x, 1, 1) + pltpu.roll(x, 255, 1))
            x = 0.2 * x + inv * (rhs + around)
        mine = jnp.where(row128 < 4, x[3:4, 0:128], x[4:5, 0:128])
        top = mine.astype(BF16).astype(F32)
        lhs[n * 8:n * 8 + 8, :] = jnp.concatenate([top, mine - top], 1)

    for m in m1 + m2:
        m.wait_send()
    for m, ds in list(zip(ms, (1, -1))) + [(m, d[1]) for m, d in zip(md, DIAG)] + [
            (m, d[1]) for m, d in zip(mb, DIRS)]:
        there(ds, m.wait_send)


def lift_kernel(live_ref, raw_ref, sm_ref, lhs, own_hbm, pred_hbm, corr_hbm, own_ref, corr, sems):
    cells = own_ref.shape[1]
    width = 256
    count = cells // width
    pred_out = pltpu.make_async_copy(raw_ref, pred_hbm, sems.at[0])
    pred_out.start()
    own_in = pltpu.make_async_copy(own_hbm, own_ref, sems.at[1])
    own_in.start()
    first = lax.axis_index("span") * (cells // FAN)
    x = lhs[...].astype(BF16)
    own_in.wait()
    live = live_ref[0, 0]
    outs = []
    for j in range(count):
        at = slice(j * width, j * width + width)
        r = lax.broadcasted_iota(jnp.int32, (256, width), 1) + j * width
        k = lax.broadcasted_iota(jnp.int32, (256, width), 0) & 127
        b = r >> 4
        e = r & (FAN - 1)
        to = jnp.where(e == 0, b - 1, jnp.where(e == FAN - 1, b + 1, -9))
        l1 = jnp.dot(x, (b == k).astype(F32).astype(BF16), preferred_element_type=F32)
        l2 = jnp.dot(x, (to == k).astype(F32).astype(BF16), preferred_element_type=F32)
        r = lax.broadcasted_iota(jnp.int32, (8, width), 1) + j * width
        f = (r < live * (cells // BLOCKS)).astype(F32)
        away = own_ref[:, at] != first + (r >> 4)
        for n in range(NT):
            k = slice(n * 8, n * 8 + 8)
            corr[k, at] = f * (sm_ref[k, at] + jnp.where(away, l2[k], l1[k]))
        if j % 2:
            at = slice(j * width - width, j * width + width)
            outs.append(pltpu.make_async_copy(corr.at[:, at], corr_hbm.at[:, at], sems.at[2 + j // 2]))
            outs[-1].start()
    for m in outs + [pred_out]:
        m.wait()


def shards(n_theta, n_span, velocity, pressure, diffusivity, live_blocks, owner_map, coarse_diag):
    ncomp, ntime, planes, cells = velocity.shape
    vmem = pl.BlockSpec(memory_space=pltpu.VMEM)
    hbm = pl.BlockSpec(memory_space=pltpu.HBM)
    smem = pl.BlockSpec(memory_space=pltpu.SMEM)
    n = len(DIRS)
    rows = ntime * planes
    pin = lambda x: pltpu.with_memory_space_constraint(x, pltpu.HBM)
    own, live = pin(owner_map), live_blocks
    raw, sm, lhs = pl.pallas_call(
        functools.partial(kernel, n_theta, n_span),
        out_shape=(
            jax.ShapeDtypeStruct((ncomp * rows, cells), F32),
            jax.ShapeDtypeStruct((rows, cells), F32),
            jax.ShapeDtypeStruct((rows, 256), F32),
        ),
        in_specs=[smem] + [hbm] * 5,
        out_specs=(vmem, vmem, vmem),
        scratch_shapes=[
            pltpu.VMEM((ncomp * rows, cells), F32),
            pltpu.VMEM((rows, cells), F32),
            pltpu.VMEM((planes, cells), F32),
            pltpu.VMEM((planes, cells), jnp.int32),
            pltpu.VMEM(coarse_diag.shape, F32),
            pltpu.VMEM((2, 48, cells), F32),
            pltpu.VMEM((2, 48, cells), F32),
            pltpu.VMEM((2, 72, 128), F32),
            pltpu.VMEM((2, 72, 128), F32),
            pltpu.VMEM((4, 16, 128), F32),
            pltpu.VMEM((4, 16, 128), F32),
            pltpu.VMEM((48, 128), F32),
            pltpu.VMEM((4, 48, 128), F32),
            pltpu.VMEM((2, 8, 128), F32),
            pltpu.VMEM((10, 8, 128), F32),
            pltpu.VMEM((72, 128), F32),
            pltpu.VMEM((208, cells), BF16),
            pltpu.VMEM((208, cells), BF16),
            pltpu.VMEM((128, cells), BF16),
            pltpu.VMEM((128, cells), BF16),
            pltpu.VMEM((2, 9, cells), F32),
            pltpu.SemaphoreType.DMA((10 + n,)),
            pltpu.SemaphoreType.DMA((10 + n,)),
            pltpu.SemaphoreType.DMA((7,)),
        ],
        compiler_params=pltpu.CompilerParams(
            collective_id=0, has_side_effects=True, vmem_limit_bytes=40 * 2**20),
    )(
        live,
        pin(velocity.reshape(ncomp * rows, cells)),
        pin(pressure.reshape(rows, cells)),
        pin(diffusivity), own, pin(coarse_diag),
    )
    pred, corr = pl.pallas_call(
        lift_kernel,
        out_shape=(
            jax.ShapeDtypeStruct((ncomp * rows, cells), F32),
            jax.ShapeDtypeStruct((rows, cells), F32),
        ),
        in_specs=[smem, vmem, vmem, vmem, hbm],
        out_specs=(hbm, hbm),
        scratch_shapes=[
            pltpu.VMEM((planes, cells), jnp.int32),
            pltpu.VMEM((rows, cells), F32),
            pltpu.SemaphoreType.DMA((8,)),
        ],
        compiler_params=pltpu.CompilerParams(vmem_limit_bytes=24 * 2**20),
    )(live, raw, sm, lhs, own)
    return pred.reshape(velocity.shape), corr.reshape(pressure.shape)


def solution(mesh):
    return jax.shard_map(
        functools.partial(shards, mesh.shape["theta"], mesh.shape["span"]),
        mesh=mesh,
        in_specs=(
            P(None, None, "theta", "span"),
            P(None, "theta", "span"),
            P("theta", "span"),
            P("theta", "span"),
            P("theta", "span"),
            P("theta", "span"),
        ),
        out_specs=(P(None, None, "theta", "span"), P(None, "theta", "span")),
        check_vma=False,
    )
```

```python
import functools
import math

import jax
import jax.numpy as jnp
import numpy as np
from jax import lax
from jax.experimental import pallas as pl
from jax.experimental.pallas import tpu as pltpu
from jax.sharding import PartitionSpec as P

MESH = pl.DeviceIdType.MESH
BLOCKS = 8
CSWEEPS = 4
NT = 9
FAN = 16
F32 = jnp.float32
BF16 = jnp.bfloat16

DIRS = [(1, 0), (-1, 0), (2, 0), (-2, 0)] + [
    (dt, ds) for ds in (1, -1) for dt in (0, 1, -1, 2, -2)
]
NEAR = [(dt, ds) for dt in (0, 1, -1) for ds in (0, 1, -1) if dt or ds]
DIAG = [(1, 1), (1, -1), (-1, 1), (-1, -1)]
FREQ = [0.15 * (-1.0) ** d / math.sin(math.pi * d / NT) for d in range(1, 5)]


def kernel(
    n_theta, n_span,
    live_ref, v_hbm, p_hbm, d_hbm, own_hbm, cd_hbm,
    pred_ref, sm_ref, lhs,
    v_ref, p_ref, d_ref, own_ref, cd_ref,
    tsend, trecv, ssend, srecv, dsend, drecv, bsend, brecv,
    psend, precv, side_ref, stay, moved, st1, st2, edge0,
    send_sem, recv_sem, load_sem,
):
    cells = v_ref.shape[1]
    cols = cells // FAN
    t, s = lax.axis_index("theta"), lax.axis_index("span")
    third = NT * 8
    loads = [pltpu.make_async_copy(v_hbm.at[third * c:third * c + third], v_ref.at[third * c:third * c + third],
                                   load_sem.at[c]) for c in range(3)]
    loads += [pltpu.make_async_copy(a, b, load_sem.at[3 + i]) for i, (a, b) in enumerate((
        (p_hbm, p_ref), (d_hbm, d_ref), (own_hbm, own_ref), (cd_hbm, cd_ref)))]
    for m in loads:
        m.start()
    tile = lambda i: pl.ds(pl.multiple_of(i * 8, 8), 8)

    def peer(dt, ds):
        return (lax.rem(t + dt + n_theta, n_theta), s + ds)

    def there(ds, act):
        if ds == 0:
            act()
        elif ds > 0:
            pl.when(s < n_span - 1)(act)
        else:
            pl.when(s > 0)(act)

    def remote(src, dst, slot, dt, ds):
        return pltpu.make_async_remote_copy(
            src_ref=src, dst_ref=dst, send_sem=send_sem.at[slot], recv_sem=recv_sem.at[slot],
            device_id=peer(dt, ds), device_id_type=MESH)

    barrier = pltpu.get_barrier_semaphore()
    for dt, ds in NEAR:
        there(ds, lambda dt=dt, ds=ds: pl.semaphore_signal(
            barrier, inc=1, device_id=peer(dt, ds), device_id_type=MESH))

    lane = lax.broadcasted_iota(jnp.int32, (1, cells), 1)
    row8 = lax.broadcasted_iota(jnp.int32, (8, 1), 0)
    lane128 = lax.broadcasted_iota(jnp.int32, (8, 128), 1)
    row128 = lax.broadcasted_iota(jnp.int32, (8, 128), 0)
    for m in loads:
        m.wait()
    fl = (lane < live_ref[0, 0] * (cells // BLOCKS)).astype(F32)
    base = s * cols + (lane >> 4)
    mv = (own_ref[...] != base).astype(F32)
    df = d_ref[...] * (0.1 * fl)

    def pack(way, row, ref, plane, count):
        for i in range(count):
            tsend[way, row + i:row + i + 1, :] = ref[8 * i + plane:8 * i + plane + 1, :]

    for way, plane in ((0, 7), (1, 0)):
        pack(way, 0, v_ref, plane, 27)
        pack(way, 27, p_ref, plane, 9)
        tsend[way, 36:37, :] = df[plane:plane + 1, :]
        tsend[way, 37:38, :] = mv[plane:plane + 1, :]
        tsend[way, 38:39, :] = fl
    for i, (dt, ds) in enumerate(DIAG):
        way = 0 if dt > 0 else 1
        c0 = cells - 128 if ds > 0 else 0
        at = 127 if ds > 0 else 0
        a0 = tsend[way, 0:9, c0:c0 + 128][:, at:at + 1]
        a1 = tsend[way, 9:18, c0:c0 + 128][:, at:at + 1]
        l9 = lax.broadcasted_iota(jnp.int32, (9, 128), 1)
        dsend[i, 0:9, :] = jnp.where(l9 == 0, a0, a1)

    pl.semaphore_wait(barrier, jnp.where((s > 0) & (s < n_span - 1), 8, 5))

    m1 = [remote(tsend.at[w, 0:32], trecv.at[w, 0:32], w, 1 - 2 * w, 0) for w in range(2)]
    m2 = [remote(tsend.at[w, 32:48], trecv.at[w, 32:48], 2 + w, 1 - 2 * w, 0) for w in range(2)]
    ms = [remote(ssend.at[w], srecv.at[w], 4 + w, 0, 1 - 2 * w) for w in range(2)]
    md = [remote(dsend.at[i], drecv.at[i], 6 + i, dt, ds) for i, (dt, ds) in enumerate(DIAG)]
    mb = [remote(bsend, brecv.at[i], 10 + i, dt, ds) if ds == 0 else
          remote(psend.at[(1 - ds) // 2], precv.at[i - 4], 10 + i, dt, ds)
          for i, (dt, ds) in enumerate(DIRS)]
    for m in m1:
        m.start()
    for m, (dt, ds) in zip(md, DIAG):
        there(ds, m.start)

    def clear(ds):
        w = 0 if ds < 0 else 1
        srecv[w] = jnp.zeros(srecv.shape[1:], F32)
        for i, (_, e) in enumerate(DIAG):
            if e == -ds:
                drecv[i] = jnp.zeros(drecv.shape[1:], F32)
        for i, (_, e) in enumerate(DIRS):
            if e == -ds:
                precv[i - 4] = jnp.zeros(precv.shape[1:], F32)

    pl.when(s == 0)(lambda: clear(-1))
    pl.when(s == n_span - 1)(lambda: clear(1))

    def a_pair(x):
        return (jnp.where(row8 == 7, 0.0, pltpu.roll(x, 7, 0)),
                jnp.where(row8 == 0, 0.0, pltpu.roll(x, 1, 0)))

    def r_pair(x):
        return (jnp.where(lane == cells - 1, 0.0, pltpu.roll(x, cells - 1, 1)),
                jnp.where(lane == 0, 0.0, pltpu.roll(x, 1, 1)))

    width = 256
    for c in range(3):
        def source(j, _):
            at = pl.ds(pl.multiple_of(j * width, width), width)
            x = [v_ref[(c * NT + n) * 8:(c * NT + n) * 8 + 8, at] for n in range(NT)]
            acc = list(x)
            for d in range(1, 5):
                for n in range(NT):
                    gap = (x[(n - d) % NT] - x[(n + d) % NT]) * (0.2 * FREQ[d - 1])
                    acc[n] = acc[n] - gap
            for n in range(NT):
                pred_ref[(c * NT + n) * 8:(c * NT + n) * 8 + 8, at] = acc[n]
            return 0

        lax.fori_loop(0, cells // width, source, 0)

        def local(n, _):
            x = v_ref[tile(c * NT + n), :]
            ap, am = a_pair(x)
            rp, rm = r_pair(x)
            out = pred_ref[tile(c * NT + n), :] - 0.1 * (x - am)
            if c < 2:
                q = p_ref[tile(n), :]
                qp, qm = a_pair(q) if c == 0 else r_pair(q)
                out = out - 0.1 * (qp - qm)
            pred_ref[tile(c * NT + n), :] = fl * out + df * (ap + am + rp + rm - 4.0 * x)
            return 0

        lax.fori_loop(0, NT, local, 0)

        if c == 0:
            for way, plane in ((0, 7), (1, 0)):
                pack(way, 39, pred_ref, plane, 9)
                m2[way].start()
        if c == 1:
            def columns(n, _):
                for way in range(2):
                    c0, at = (cells - 128, 127) if way == 0 else (0, 0)
                    got = jnp.zeros((8, 128), F32)
                    for f, x in enumerate((
                        v_ref[tile(n), c0:c0 + 128], v_ref[tile(NT + n), c0:c0 + 128],
                        v_ref[tile(2 * NT + n), c0:c0 + 128], p_ref[tile(n), c0:c0 + 128],
                        pred_ref[tile(NT + n), c0:c0 + 128], df[:, c0:c0 + 128],
                        jnp.broadcast_to(fl[:, c0:c0 + 128], (8, 128)))):
                        got = jnp.where(lane128 == f, x[:, at:at + 1], got)
                    ssend[way, tile(n), :] = got
                return 0

            lax.fori_loop(0, NT, columns, 0)
            for m, ds in zip(ms, (1, -1)):
                there(ds, m.start)

    def members(j, _):
        at = pl.ds(pl.multiple_of(j * width, width), width)
        r = lax.broadcasted_iota(jnp.int32, (128, width), 1) + j * width
        k = lax.broadcasted_iota(jnp.int32, (128, width), 0)
        b = r >> 4
        e = r & (FAN - 1)
        to = jnp.where(e == 0, b - 1, jnp.where(e == FAN - 1, b + 1, -9))
        st1[:, at] = (b == k).astype(F32).astype(BF16)
        st2[:, at] = (to == k).astype(F32).astype(BF16)
        return 0

    lax.fori_loop(0, cells // width, members, 0)

    for m in m1 + m2:
        m.wait_recv()
    for m, (dt, ds) in zip(md, DIAG):
        there(-ds, m.wait_recv)
    for m, ds in zip(ms, (1, -1)):
        there(-ds, m.wait_recv)

    df_dn, fl_dn = trecv[0, 36:37, :], trecv[0, 38:39, :]
    df_up, fl_up = trecv[1, 36:37, :], trecv[1, 38:39, :]
    lo, hi = lane == 0, lane == cells - 1
    edge0[0] = (trecv[0, 39:48, :] + df_dn * tsend[1, 0:9, :] - 0.1 * fl_dn * tsend[1, 27:36, :]
                + jnp.where(lo, df_dn * drecv[0, 0:9, 0:1], 0.0)
                + jnp.where(hi, df_dn * drecv[1, 0:9, 0:1], 0.0))
    edge0[1] = (trecv[1, 39:48, :] + (df_up + 0.1 * fl_up) * tsend[0, 0:9, :]
                + 0.1 * fl_up * tsend[0, 27:36, :]
                + jnp.where(lo, df_up * drecv[2, 0:9, 0:1], 0.0)
                + jnp.where(hi, df_up * drecv[3, 0:9, 0:1], 0.0))
    w_dn = jnp.where(row8 == 0, df + 0.1 * fl, 0.0)
    w_up = jnp.where(row8 == 7, df, 0.0)
    q_dn = jnp.where(row8 == 0, 0.1 * fl, 0.0)
    q_up = jnp.where(row8 == 7, 0.1 * fl, 0.0)

    def completed(n, c, left, right):
        i = c * NT + n
        out = (pred_ref[tile(i), :] + w_dn * trecv[0, pl.ds(i, 1), :]
               + w_up * trecv[1, pl.ds(i, 1), :])
        if c == 0:
            out = (out + q_dn * trecv[0, pl.ds(27 + n, 1), :]
                   - q_up * trecv[1, pl.ds(27 + n, 1), :])
        ends = []
        for c0, col, side, sign in ((0, 0, left, 0.1), (cells - 128, 127, right, -0.1)):
            at = slice(c0, c0 + 128)
            x = df[:, at] * side[:, c:c + 1]
            if c == 1:
                x = x + sign * fl[:, at] * side[:, 3:4]
            ends.append(out[:, at] + jnp.where(lane128 == col, x, 0.0))
        out = jnp.concatenate([ends[0], out[:, 128:cells - 128], ends[1]], 1)
        pred_ref[tile(i), :] = out
        return out

    def complete(n, _):
        left, right = srecv[0, tile(n), :], srecv[1, tile(n), :]
        first = completed(n, 0, left, right)
        second = completed(n, 1, left, right)
        fp = jnp.where(row8 == 7, edge0[1, pl.ds(n, 1), :], pltpu.roll(first, 7, 0))
        fm = jnp.where(row8 == 0, edge0[0, pl.ds(n, 1), :], pltpu.roll(first, 1, 0))
        x = [v_ref[tile(NT + n), 0:128][:, 0:1],
             v_ref[tile(NT + n), cells - 128:cells][:, 127:128]]
        q = [p_ref[tile(n), 0:128][:, 0:1], p_ref[tile(n), cells - 128:cells][:, 127:128]]
        rows = pl.ds(n, 1)

        def corner(side, dn, up):
            return (jnp.where(row8 == 0, (side[:, 5:6] + 0.1 * side[:, 6:7]) * drecv[dn, rows, :][:, 1:2], 0.0)
                    + jnp.where(row8 == 7, side[:, 5:6] * drecv[up, rows, :][:, 1:2], 0.0))

        pl1 = (left[:, 4:5] + left[:, 5:6] * x[0] - 0.1 * left[:, 6:7] * q[0]
               + corner(left, 0, 2))
        pr1 = (right[:, 4:5] + right[:, 5:6] * x[1] + 0.1 * right[:, 6:7] * q[1]
               + corner(right, 1, 3))
        sp = jnp.where(hi, pr1, pltpu.roll(second, cells - 1, 1))
        sn = jnp.where(lo, pl1, pltpu.roll(second, 1, 1))
        sm = 0.1 * fl * (fp - fm + sp - sn)
        sm_ref[tile(n), :] = sm
        ap, am = a_pair(sm)
        rp, rm = r_pair(sm)
        rem = fl * (sm + (ap + am + rp + rm))
        gone = rem * mv
        kept = rem - gone
        at = pl.ds(pl.multiple_of(n * 16, 16), 16)
        for ref, x in ((stay, kept), (moved, gone)):
            top = x.astype(BF16).astype(F32)
            ref[at, :] = jnp.concatenate([top, x - top], 0).astype(BF16)
        e = jnp.where(lane128 == 0, sm[:, cells - 1:cells],
                      jnp.where(lane128 == 127, sm[:, 0:1] * left[:, 6:7], 0.0))
        e0 = jnp.sum(e[0:4], axis=0, keepdims=True)
        e1 = jnp.sum(e[4:8], axis=0, keepdims=True)
        side_ref[tile(n), :] = jnp.where(row128 == 5, e0, jnp.where(row128 == 6, e1, 0.0))
        return 0

    lax.fori_loop(0, NT, complete, 0, unroll=3)

    def pieces(x):
        top = x.astype(BF16).astype(F32)
        return [top, x - top]

    zero7 = jnp.zeros((7, cells), F32)
    kept, gone = [], []
    for w, plane in ((0, 0), (1, 7)):
        x = jnp.concatenate([sm_ref[8 * i + plane:8 * i + plane + 1, :] for i in range(NT)], 0)
        x = x * trecv[w, 38:39, :]
        g = x * trecv[w, 37:38, :]
        for rows, y in ((kept, x - g), (gone, g)):
            for z in pieces(y):
                rows += [z, zero7]
    for ref, rows in ((stay, kept), (moved, gone)):
        for i in range(4):
            at = 16 * NT + 16 * i
            ref[at:at + 16, :] = jnp.concatenate(rows[2 * i:2 * i + 2], 0).astype(BF16)

    nt = (((1,), (1,)), ((), ()))
    tot = (lax.dot_general(stay[...], st1[...], nt, preferred_element_type=F32)
           + lax.dot_general(moved[...], st2[...], nt, preferred_element_type=F32))
    e_dn = tot[16 * NT:16 * NT + 16] + tot[16 * NT + 16:16 * NT + 32]
    e_up = tot[16 * NT + 32:16 * NT + 48] + tot[16 * NT + 48:16 * NT + 64]
    pack_r, pack_l = jnp.zeros((8, 128), F32), jnp.zeros((8, 128), F32)
    main, sides = [], jnp.zeros((8, 128), F32)
    for n in range(NT):
        x = tot[16 * n:16 * n + 8] + tot[16 * n + 8:16 * n + 16]
        x0 = jnp.sum(x[0:4], axis=0, keepdims=True)
        x1 = jnp.sum(x[4:8], axis=0, keepdims=True)
        x = jnp.where(row128 == 0, e_dn[n:n + 1], jnp.where(row128 == 1, x0, jnp.where(
            row128 == 2, x1, jnp.where(row128 == 3, e_up[n:n + 1], side_ref[n * 8:n * 8 + 8, :]))))
        main.append(x)
        slot = (lane128 >> 2) == n
        pack_r = jnp.where(slot, pltpu.roll(x, 3 + 4 * n, 1), pack_r)
        pack_l = jnp.where(slot, pltpu.roll(x, 1 + 4 * n, 1), pack_l)
        sides = jnp.where((lane128 >> 1) == n, pltpu.roll(x, 1 + 2 * n, 1), sides)
    cd = jnp.concatenate([cd_ref[...], jnp.zeros((6, 128), F32)], 0)
    for i in range(5):
        y = main[2 * i + 1] if 2 * i + 1 < NT else jnp.zeros((8, 128), F32)
        bsend[8 * i:8 * i + 8, :] = jnp.where(row128 < 4, main[2 * i], pltpu.roll(y, 4, 0))
    bsend[40:48, :] = jnp.where(row128 < 4, cd, sides)
    cslot = (lane128 >> 2) == 10
    psend[0] = jnp.where(cslot, pltpu.roll(cd, 43, 1), pack_r)
    psend[1] = jnp.where(cslot, pltpu.roll(cd, 41, 1), pack_l)
    for m, (dt, ds) in sorted(zip(mb, DIRS), key=lambda x: -abs(x[1][0]) - abs(x[1][1])):
        there(ds, m.start)

    def third_component(n, _):
        completed(n, 2, srecv[0, tile(n), :], srecv[1, tile(n), :])
        return 0

    lax.fori_loop(0, NT, third_component, 0)
    for m, (dt, ds) in zip(mb, DIRS):
        there(-ds, m.wait_recv)

    def keep(x, rows):
        return jnp.where((row128 >= rows[0]) & (row128 < rows[1]), x, 0.0)

    def turn(x, by, axis):
        return pltpu.roll(x, by % x.shape[axis], axis) if by % x.shape[axis] else x

    def rows_of(ot):
        return (2, 4) if ot == -2 else (0, 2) if ot == 2 else (0, 4)

    def diag_rows(x, ot):
        return turn(keep(x, (1, 2) if ot == -2 else (0, 1) if ot == 2 else (0, 2)), 3 + 2 * ot, 0)

    near = [(0, bsend)] + [(-dt, brecv.at[i]) for i, (dt, ds) in enumerate(DIRS) if ds == 0]
    d0 = sum(diag_rows(ref[40:48, :], ot) for ot, ref in near)
    beside = []
    for sent in (1, -1):
        got = [(-dt, precv[i - 4]) for i, (dt, ds) in enumerate(DIRS) if ds == sent]
        beside.append((
            sum(turn(keep(x, rows_of(ot)), 2 * ot + 2, 0) for ot, x in got),
            sum(turn(keep(x, (rows_of(ot)[0] + 4, rows_of(ot)[1] + 4)), 2 * ot + 6, 0) for ot, x in got),
            sum(diag_rows(x, ot) for ot, x in got)))
    s_near = sum(turn(keep(ref[40:48, :], (rows_of(ot)[0] + 4, rows_of(ot)[1] + 4)), 2 * ot + 6, 0)
                 for ot, ref in near)
    (ml, sl, dl), (mr, sr, dr) = beside
    from_left, from_right = lane128 >= 125, lane128 <= 2
    d1 = (jnp.where(from_left, turn(dl, -43, 1), 0.0) + jnp.where(from_right, turn(dr, -41, 1), 0.0))
    ok = jnp.where(lane128 >= 64, (s > 0).astype(F32), (s < n_span - 1).astype(F32))
    inv = jnp.concatenate([0.8 / (4.0 + d0), ok * 0.8 / (4.0 + d1)], 1)
    for n in range(NT):
        lo4 = 4 * (n % 2)
        r0 = sum(turn(keep(ref[8 * (n // 2):8 * (n // 2) + 8, :], (rows_of(ot)[0] + lo4, rows_of(ot)[1] + lo4)),
                      2 * ot + 2 - lo4, 0) for ot, ref in near)
        r0 = r0 + jnp.where(lane128 == 0, turn(sl, -(3 + 4 * n), 1), 0.0)
        r0 = r0 + jnp.where(lane128 == 127, turn(sr, -(1 + 4 * n), 1), 0.0)
        r1 = jnp.where((lane128 == 0) | (lane128 == 127), turn(s_near, -(1 + 2 * n), 1), 0.0)
        r1 = r1 + jnp.where(from_left, turn(ml, -(3 + 4 * n), 1), 0.0)
        r1 = r1 + jnp.where(from_right, turn(mr, -(1 + 4 * n), 1), 0.0)
        rhs = jnp.concatenate([r0, r1], 1)
        x = inv * rhs
        for _ in range(CSWEEPS - 1):
            around = (pltpu.roll(x, 1, 0) + pltpu.roll(x, 7, 0)
                      + pltpu.roll(x, 1, 1) + pltpu.roll(x, 255, 1))
            x = 0.2 * x + inv * (rhs + around)
        mine = jnp.where(row128 < 4, x[3:4, 0:128], x[4:5, 0:128])
        top = mine.astype(BF16).astype(F32)
        lhs[n * 8:n * 8 + 8, :] = jnp.concatenate([top, mine - top], 1)

    for m in m1 + m2:
        m.wait_send()
    for m, ds in list(zip(ms, (1, -1))) + [(m, d[1]) for m, d in zip(md, DIAG)] + [
            (m, d[1]) for m, d in zip(mb, DIRS)]:
        there(ds, m.wait_send)


def lift_kernel(live_ref, raw_ref, sm_ref, lhs, own_hbm, pred_hbm, corr_hbm, own_ref, corr, sems):
    cells = own_ref.shape[1]
    width = 256
    count = cells // width
    pred_out = pltpu.make_async_copy(raw_ref, pred_hbm, sems.at[0])
    pred_out.start()
    own_in = pltpu.make_async_copy(own_hbm, own_ref, sems.at[1])
    own_in.start()
    first = lax.axis_index("span") * (cells // FAN)
    x = lhs[...].astype(BF16)
    own_in.wait()
    live = live_ref[0, 0]
    outs = []
    for j in range(count):
        at = slice(j * width, j * width + width)
        r = lax.broadcasted_iota(jnp.int32, (256, width), 1) + j * width
        k = lax.broadcasted_iota(jnp.int32, (256, width), 0) & 127
        b = r >> 4
        e = r & (FAN - 1)
        to = jnp.where(e == 0, b - 1, jnp.where(e == FAN - 1, b + 1, -9))
        l1 = jnp.dot(x, (b == k).astype(F32).astype(BF16), preferred_element_type=F32)
        l2 = jnp.dot(x, (to == k).astype(F32).astype(BF16), preferred_element_type=F32)
        r = lax.broadcasted_iota(jnp.int32, (8, width), 1) + j * width
        f = (r < live * (cells // BLOCKS)).astype(F32)
        away = own_ref[:, at] != first + (r >> 4)
        for n in range(NT):
            k = slice(n * 8, n * 8 + 8)
            corr[k, at] = f * (sm_ref[k, at] + jnp.where(away, l2[k], l1[k]))
        if j % 2:
            at = slice(j * width - width, j * width + width)
            outs.append(pltpu.make_async_copy(corr.at[:, at], corr_hbm.at[:, at], sems.at[2 + j // 2]))
            outs[-1].start()
    for m in outs + [pred_out]:
        m.wait()


def shards(n_theta, n_span, velocity, pressure, diffusivity, live_blocks, owner_map, coarse_diag):
    ncomp, ntime, planes, cells = velocity.shape
    vmem = pl.BlockSpec(memory_space=pltpu.VMEM)
    hbm = pl.BlockSpec(memory_space=pltpu.HBM)
    smem = pl.BlockSpec(memory_space=pltpu.SMEM)
    n = len(DIRS)
    rows = ntime * planes
    pin = lambda x: pltpu.with_memory_space_constraint(x, pltpu.HBM)
    own, live = pin(owner_map), live_blocks
    raw, sm, lhs = pl.pallas_call(
        functools.partial(kernel, n_theta, n_span),
        out_shape=(
            jax.ShapeDtypeStruct((ncomp * rows, cells), F32),
            jax.ShapeDtypeStruct((rows, cells), F32),
            jax.ShapeDtypeStruct((rows, 256), F32),
        ),
        in_specs=[smem] + [hbm] * 5,
        out_specs=(vmem, vmem, vmem),
        scratch_shapes=[
            pltpu.VMEM((ncomp * rows, cells), F32),
            pltpu.VMEM((rows, cells), F32),
            pltpu.VMEM((planes, cells), F32),
            pltpu.VMEM((planes, cells), jnp.int32),
            pltpu.VMEM(coarse_diag.shape, F32),
            pltpu.VMEM((2, 48, cells), F32),
            pltpu.VMEM((2, 48, cells), F32),
            pltpu.VMEM((2, 72, 128), F32),
            pltpu.VMEM((2, 72, 128), F32),
            pltpu.VMEM((4, 16, 128), F32),
            pltpu.VMEM((4, 16, 128), F32),
            pltpu.VMEM((48, 128), F32),
            pltpu.VMEM((4, 48, 128), F32),
            pltpu.VMEM((2, 8, 128), F32),
            pltpu.VMEM((10, 8, 128), F32),
            pltpu.VMEM((72, 128), F32),
            pltpu.VMEM((208, cells), BF16),
            pltpu.VMEM((208, cells), BF16),
            pltpu.VMEM((128, cells), BF16),
            pltpu.VMEM((128, cells), BF16),
            pltpu.VMEM((2, 9, cells), F32),
            pltpu.SemaphoreType.DMA((10 + n,)),
            pltpu.SemaphoreType.DMA((10 + n,)),
            pltpu.SemaphoreType.DMA((7,)),
        ],
        compiler_params=pltpu.CompilerParams(
            collective_id=0, has_side_effects=True, vmem_limit_bytes=40 * 2**20),
    )(
        live,
        pin(velocity.reshape(ncomp * rows, cells)),
        pin(pressure.reshape(rows, cells)),
        pin(diffusivity), own, pin(coarse_diag),
    )
    pred, corr = pl.pallas_call(
        lift_kernel,
        out_shape=(
            jax.ShapeDtypeStruct((ncomp * rows, cells), F32),
            jax.ShapeDtypeStruct((rows, cells), F32),
        ),
        in_specs=[smem, vmem, vmem, vmem, hbm],
        out_specs=(hbm, hbm),
        scratch_shapes=[
            pltpu.VMEM((planes, cells), jnp.int32),
            pltpu.VMEM((rows, cells), F32),
            pltpu.SemaphoreType.DMA((8,)),
        ],
        compiler_params=pltpu.CompilerParams(vmem_limit_bytes=24 * 2**20),
    )(live, raw, sm, lhs, own)
    return pred.reshape(velocity.shape), corr.reshape(pressure.shape)


def solution(mesh):
    return jax.shard_map(
        functools.partial(shards, mesh.shape["theta"], mesh.shape["span"]),
        mesh=mesh,
        in_specs=(
            P(None, None, "theta", "span"),
            P(None, "theta", "span"),
            P("theta", "span"),
            P("theta", "span"),
            P("theta", "span"),
            P("theta", "span"),
        ),
        out_specs=(P(None, None, "theta", "span"), P(None, "theta", "span")),
        check_vma=False,
    )
```

```python
import functools
import math

import jax
import jax.numpy as jnp
import numpy as np
from jax import lax
from jax.experimental import pallas as pl
from jax.experimental.pallas import tpu as pltpu
from jax.sharding import PartitionSpec as P

MESH = pl.DeviceIdType.MESH
BLOCKS = 8
CSWEEPS = 4
NT = 9
FAN = 16
F32 = jnp.float32
BF16 = jnp.bfloat16

DIRS = [(1, 0), (-1, 0), (2, 0), (-2, 0)] + [
    (dt, ds) for ds in (1, -1) for dt in (0, 1, -1, 2, -2)
]
NEAR = [(dt, ds) for dt in (0, 1, -1) for ds in (0, 1, -1) if dt or ds]
DIAG = [(1, 1), (1, -1), (-1, 1), (-1, -1)]
FREQ = [0.15 * (-1.0) ** d / math.sin(math.pi * d / NT) for d in range(1, 5)]


def kernel(
    n_theta, n_span,
    live_ref, v_hbm, p_hbm, d_hbm, own_hbm, cd_hbm,
    pred_ref, sm_ref, lhs,
    v_ref, p_ref, d_ref, own_ref, cd_ref,
    tsend, trecv, ssend, srecv, dsend, drecv, bsend, brecv,
    psend, precv, side_ref, stay, moved, st1, st2, edge0,
    send_sem, recv_sem, load_sem,
):
    cells = v_ref.shape[1]
    cols = cells // FAN
    t, s = lax.axis_index("theta"), lax.axis_index("span")
    third = NT * 8
    loads = [pltpu.make_async_copy(v_hbm.at[third * c:third * c + third], v_ref.at[third * c:third * c + third],
                                   load_sem.at[c]) for c in range(3)]
    loads += [pltpu.make_async_copy(a, b, load_sem.at[3 + i]) for i, (a, b) in enumerate((
        (p_hbm, p_ref), (d_hbm, d_ref), (own_hbm, own_ref), (cd_hbm, cd_ref)))]
    for m in loads:
        m.start()
    tile = lambda i: pl.ds(pl.multiple_of(i * 8, 8), 8)

    def peer(dt, ds):
        return (lax.rem(t + dt + n_theta, n_theta), s + ds)

    def there(ds, act):
        if ds == 0:
            act()
        elif ds > 0:
            pl.when(s < n_span - 1)(act)
        else:
            pl.when(s > 0)(act)

    def remote(src, dst, slot, dt, ds):
        return pltpu.make_async_remote_copy(
            src_ref=src, dst_ref=dst, send_sem=send_sem.at[slot], recv_sem=recv_sem.at[slot],
            device_id=peer(dt, ds), device_id_type=MESH)

    barrier = pltpu.get_barrier_semaphore()
    for dt, ds in NEAR:
        there(ds, lambda dt=dt, ds=ds: pl.semaphore_signal(
            barrier, inc=1, device_id=peer(dt, ds), device_id_type=MESH))

    lane = lax.broadcasted_iota(jnp.int32, (1, cells), 1)
    row8 = lax.broadcasted_iota(jnp.int32, (8, 1), 0)
    lane128 = lax.broadcasted_iota(jnp.int32, (8, 128), 1)
    row128 = lax.broadcasted_iota(jnp.int32, (8, 128), 0)
    for m in loads:
        m.wait()
    fl = (lane < live_ref[0, 0] * (cells // BLOCKS)).astype(F32)
    base = s * cols + (lane >> 4)
    mv = (own_ref[...] != base).astype(F32)
    df = d_ref[...] * (0.1 * fl)

    def pack(way, row, ref, plane, count, first=0):
        for i in range(count):
            at = 8 * (first + i) + plane
            tsend[way, row + i:row + i + 1, :] = ref[at:at + 1, :]

    for way, plane in ((0, 7), (1, 0)):
        pack(way, 0, v_ref, plane, 18)
        pack(way, 18, p_ref, plane, 9)
        pack(way, 39, v_ref, plane, 9, 18)
        tsend[way, 27:28, :] = df[plane:plane + 1, :]
        tsend[way, 28:29, :] = mv[plane:plane + 1, :]
        tsend[way, 29:30, :] = fl
    for i, (dt, ds) in enumerate(DIAG):
        way = 0 if dt > 0 else 1
        c0 = cells - 128 if ds > 0 else 0
        at = 127 if ds > 0 else 0
        a0 = tsend[way, 0:9, c0:c0 + 128][:, at:at + 1]
        a1 = tsend[way, 9:18, c0:c0 + 128][:, at:at + 1]
        l9 = lax.broadcasted_iota(jnp.int32, (9, 128), 1)
        dsend[i, 0:9, :] = jnp.where(l9 == 0, a0, a1)

    pl.semaphore_wait(barrier, jnp.where((s > 0) & (s < n_span - 1), 8, 5))

    m1 = [remote(tsend.at[w, 0:24], trecv.at[w, 0:24], w, 1 - 2 * w, 0) for w in range(2)]
    m2 = [remote(tsend.at[w, 24:40], trecv.at[w, 24:40], 2 + w, 1 - 2 * w, 0) for w in range(2)]
    last = 10 + len(DIRS)
    m3 = [remote(tsend.at[w, 40:48], trecv.at[w, 40:48], last + w, 1 - 2 * w, 0) for w in range(2)]
    ms = [remote(ssend.at[w], srecv.at[w], 4 + w, 0, 1 - 2 * w) for w in range(2)]
    md = [remote(dsend.at[i], drecv.at[i], 6 + i, dt, ds) for i, (dt, ds) in enumerate(DIAG)]
    mb = [remote(bsend, brecv.at[i], 10 + i, dt, ds) if ds == 0 else
          remote(psend.at[(1 - ds) // 2], precv.at[i - 4], 10 + i, dt, ds)
          for i, (dt, ds) in enumerate(DIRS)]
    for m in m1:
        m.start()
    for m, (dt, ds) in zip(md, DIAG):
        there(ds, m.start)

    def clear(ds):
        w = 0 if ds < 0 else 1
        srecv[w] = jnp.zeros(srecv.shape[1:], F32)
        for i, (_, e) in enumerate(DIAG):
            if e == -ds:
                drecv[i] = jnp.zeros(drecv.shape[1:], F32)
        for i, (_, e) in enumerate(DIRS):
            if e == -ds:
                precv[i - 4] = jnp.zeros(precv.shape[1:], F32)

    pl.when(s == 0)(lambda: clear(-1))
    pl.when(s == n_span - 1)(lambda: clear(1))

    def a_pair(x):
        return (jnp.where(row8 == 7, 0.0, pltpu.roll(x, 7, 0)),
                jnp.where(row8 == 0, 0.0, pltpu.roll(x, 1, 0)))

    def r_pair(x):
        return (jnp.where(lane == cells - 1, 0.0, pltpu.roll(x, cells - 1, 1)),
                jnp.where(lane == 0, 0.0, pltpu.roll(x, 1, 1)))

    width = 256
    for c in range(3):
        def source(j, _):
            at = pl.ds(pl.multiple_of(j * width, width), width)
            x = [v_ref[(c * NT + n) * 8:(c * NT + n) * 8 + 8, at] for n in range(NT)]
            acc = list(x)
            for d in range(1, 5):
                for n in range(NT):
                    gap = (x[(n - d) % NT] - x[(n + d) % NT]) * (0.2 * FREQ[d - 1])
                    acc[n] = acc[n] - gap
            for n in range(NT):
                pred_ref[(c * NT + n) * 8:(c * NT + n) * 8 + 8, at] = acc[n]
            return 0

        lax.fori_loop(0, cells // width, source, 0)

        def local(n, _):
            x = v_ref[tile(c * NT + n), :]
            ap, am = a_pair(x)
            rp, rm = r_pair(x)
            out = pred_ref[tile(c * NT + n), :] - 0.1 * (x - am)
            if c < 2:
                q = p_ref[tile(n), :]
                qp, qm = a_pair(q) if c == 0 else r_pair(q)
                out = out - 0.1 * (qp - qm)
            pred_ref[tile(c * NT + n), :] = fl * out + df * (ap + am + rp + rm - 4.0 * x)
            return 0

        lax.fori_loop(0, NT, local, 0)

        if c == 0:
            for way, plane in ((0, 7), (1, 0)):
                pack(way, 30, pred_ref, plane, 9)
                m2[way].start()
        if c == 1:
            def columns(n, _):
                for way in range(2):
                    c0, at = (cells - 128, 127) if way == 0 else (0, 0)
                    got = jnp.zeros((8, 128), F32)
                    for f, x in enumerate((
                        v_ref[tile(n), c0:c0 + 128], v_ref[tile(NT + n), c0:c0 + 128],
                        v_ref[tile(2 * NT + n), c0:c0 + 128], p_ref[tile(n), c0:c0 + 128],
                        pred_ref[tile(NT + n), c0:c0 + 128], df[:, c0:c0 + 128],
                        jnp.broadcast_to(fl[:, c0:c0 + 128], (8, 128)))):
                        got = jnp.where(lane128 == f, x[:, at:at + 1], got)
                    ssend[way, tile(n), :] = got
                return 0

            lax.fori_loop(0, NT, columns, 0)
            for m, ds in zip(ms, (1, -1)):
                there(ds, m.start)

    def members(j, _):
        at = pl.ds(pl.multiple_of(j * width, width), width)
        r = lax.broadcasted_iota(jnp.int32, (128, width), 1) + j * width
        k = lax.broadcasted_iota(jnp.int32, (128, width), 0)
        b = r >> 4
        e = r & (FAN - 1)
        to = jnp.where(e == 0, b - 1, jnp.where(e == FAN - 1, b + 1, -9))
        st1[:, at] = (b == k).astype(F32).astype(BF16)
        st2[:, at] = (to == k).astype(F32).astype(BF16)
        return 0

    lax.fori_loop(0, cells // width, members, 0)

    for m in m1 + m2:
        m.wait_recv()
    for m in m3:
        m.start()
    for m, (dt, ds) in zip(md, DIAG):
        there(-ds, m.wait_recv)
    for m, ds in zip(ms, (1, -1)):
        there(-ds, m.wait_recv)

    df_dn, fl_dn = trecv[0, 27:28, :], trecv[0, 29:30, :]
    df_up, fl_up = trecv[1, 27:28, :], trecv[1, 29:30, :]
    lo, hi = lane == 0, lane == cells - 1
    edge0[0] = (trecv[0, 30:39, :] + df_dn * tsend[1, 0:9, :] - 0.1 * fl_dn * tsend[1, 18:27, :]
                + jnp.where(lo, df_dn * drecv[0, 0:9, 0:1], 0.0)
                + jnp.where(hi, df_dn * drecv[1, 0:9, 0:1], 0.0))
    edge0[1] = (trecv[1, 30:39, :] + (df_up + 0.1 * fl_up) * tsend[0, 0:9, :]
                + 0.1 * fl_up * tsend[0, 18:27, :]
                + jnp.where(lo, df_up * drecv[2, 0:9, 0:1], 0.0)
                + jnp.where(hi, df_up * drecv[3, 0:9, 0:1], 0.0))
    w_dn = jnp.where(row8 == 0, df + 0.1 * fl, 0.0)
    w_up = jnp.where(row8 == 7, df, 0.0)
    q_dn = jnp.where(row8 == 0, 0.1 * fl, 0.0)
    q_up = jnp.where(row8 == 7, 0.1 * fl, 0.0)

    def completed(n, c, left, right):
        i = c * NT + n
        halo = pl.ds(i if c < 2 else 39 + n, 1)
        out = pred_ref[tile(i), :] + w_dn * trecv[0, halo, :] + w_up * trecv[1, halo, :]
        if c == 0:
            out = (out + q_dn * trecv[0, pl.ds(18 + n, 1), :]
                   - q_up * trecv[1, pl.ds(18 + n, 1), :])
        ends = []
        for c0, col, side, sign in ((0, 0, left, 0.1), (cells - 128, 127, right, -0.1)):
            at = slice(c0, c0 + 128)
            x = df[:, at] * side[:, c:c + 1]
            if c == 1:
                x = x + sign * fl[:, at] * side[:, 3:4]
            ends.append(out[:, at] + jnp.where(lane128 == col, x, 0.0))
        out = jnp.concatenate([ends[0], out[:, 128:cells - 128], ends[1]], 1)
        pred_ref[tile(i), :] = out
        return out

    def complete(n, _):
        left, right = srecv[0, tile(n), :], srecv[1, tile(n), :]
        first = completed(n, 0, left, right)
        second = completed(n, 1, left, right)
        fp = jnp.where(row8 == 7, edge0[1, pl.ds(n, 1), :], pltpu.roll(first, 7, 0))
        fm = jnp.where(row8 == 0, edge0[0, pl.ds(n, 1), :], pltpu.roll(first, 1, 0))
        x = [v_ref[tile(NT + n), 0:128][:, 0:1],
             v_ref[tile(NT + n), cells - 128:cells][:, 127:128]]
        q = [p_ref[tile(n), 0:128][:, 0:1], p_ref[tile(n), cells - 128:cells][:, 127:128]]
        rows = pl.ds(n, 1)

        def corner(side, dn, up):
            return (jnp.where(row8 == 0, (side[:, 5:6] + 0.1 * side[:, 6:7]) * drecv[dn, rows, :][:, 1:2], 0.0)
                    + jnp.where(row8 == 7, side[:, 5:6] * drecv[up, rows, :][:, 1:2], 0.0))

        pl1 = (left[:, 4:5] + left[:, 5:6] * x[0] - 0.1 * left[:, 6:7] * q[0]
               + corner(left, 0, 2))
        pr1 = (right[:, 4:5] + right[:, 5:6] * x[1] + 0.1 * right[:, 6:7] * q[1]
               + corner(right, 1, 3))
        sp = jnp.where(hi, pr1, pltpu.roll(second, cells - 1, 1))
        sn = jnp.where(lo, pl1, pltpu.roll(second, 1, 1))
        sm = 0.1 * fl * (fp - fm + sp - sn)
        sm_ref[tile(n), :] = sm
        ap, am = a_pair(sm)
        rp, rm = r_pair(sm)
        rem = fl * (sm + (ap + am + rp + rm))
        gone = rem * mv
        kept = rem - gone
        at = pl.ds(pl.multiple_of(n * 16, 16), 16)
        for ref, x in ((stay, kept), (moved, gone)):
            top = x.astype(BF16).astype(F32)
            ref[at, :] = jnp.concatenate([top, x - top], 0).astype(BF16)
        e = jnp.where(lane128 == 0, sm[:, cells - 1:cells],
                      jnp.where(lane128 == 127, sm[:, 0:1] * left[:, 6:7], 0.0))
        e0 = jnp.sum(e[0:4], axis=0, keepdims=True)
        e1 = jnp.sum(e[4:8], axis=0, keepdims=True)
        side_ref[tile(n), :] = jnp.where(row128 == 5, e0, jnp.where(row128 == 6, e1, 0.0))
        return 0

    lax.fori_loop(0, NT, complete, 0, unroll=3)

    def pieces(x):
        top = x.astype(BF16).astype(F32)
        return [top, x - top]

    zero7 = jnp.zeros((7, cells), F32)
    kept, gone = [], []
    for w, plane in ((0, 0), (1, 7)):
        x = jnp.concatenate([sm_ref[8 * i + plane:8 * i + plane + 1, :] for i in range(NT)], 0)
        x = x * trecv[w, 29:30, :]
        g = x * trecv[w, 28:29, :]
        for rows, y in ((kept, x - g), (gone, g)):
            for z in pieces(y):
                rows += [z, zero7]
    for ref, rows in ((stay, kept), (moved, gone)):
        for i in range(4):
            at = 16 * NT + 16 * i
            ref[at:at + 16, :] = jnp.concatenate(rows[2 * i:2 * i + 2], 0).astype(BF16)

    nt = (((1,), (1,)), ((), ()))
    tot = (lax.dot_general(stay[...], st1[...], nt, preferred_element_type=F32)
           + lax.dot_general(moved[...], st2[...], nt, preferred_element_type=F32))
    e_dn = tot[16 * NT:16 * NT + 16] + tot[16 * NT + 16:16 * NT + 32]
    e_up = tot[16 * NT + 32:16 * NT + 48] + tot[16 * NT + 48:16 * NT + 64]
    pack_r, pack_l = jnp.zeros((8, 128), F32), jnp.zeros((8, 128), F32)
    main, sides = [], jnp.zeros((8, 128), F32)
    for n in range(NT):
        x = tot[16 * n:16 * n + 8] + tot[16 * n + 8:16 * n + 16]
        x0 = jnp.sum(x[0:4], axis=0, keepdims=True)
        x1 = jnp.sum(x[4:8], axis=0, keepdims=True)
        x = jnp.where(row128 == 0, e_dn[n:n + 1], jnp.where(row128 == 1, x0, jnp.where(
            row128 == 2, x1, jnp.where(row128 == 3, e_up[n:n + 1], side_ref[n * 8:n * 8 + 8, :]))))
        main.append(x)
        slot = (lane128 >> 2) == n
        pack_r = jnp.where(slot, pltpu.roll(x, 3 + 4 * n, 1), pack_r)
        pack_l = jnp.where(slot, pltpu.roll(x, 1 + 4 * n, 1), pack_l)
        sides = jnp.where((lane128 >> 1) == n, pltpu.roll(x, 1 + 2 * n, 1), sides)
    cd = jnp.concatenate([cd_ref[...], jnp.zeros((6, 128), F32)], 0)
    for i in range(5):
        y = main[2 * i + 1] if 2 * i + 1 < NT else jnp.zeros((8, 128), F32)
        bsend[8 * i:8 * i + 8, :] = jnp.where(row128 < 4, main[2 * i], pltpu.roll(y, 4, 0))
    bsend[40:48, :] = jnp.where(row128 < 4, cd, sides)
    cslot = (lane128 >> 2) == 10
    psend[0] = jnp.where(cslot, pltpu.roll(cd, 43, 1), pack_r)
    psend[1] = jnp.where(cslot, pltpu.roll(cd, 41, 1), pack_l)
    for m, (dt, ds) in sorted(zip(mb, DIRS), key=lambda x: -abs(x[1][0]) - abs(x[1][1])):
        there(ds, m.start)

    def third_component(n, _):
        completed(n, 2, srecv[0, tile(n), :], srecv[1, tile(n), :])
        return 0

    for m in m3:
        m.wait_recv()
    lax.fori_loop(0, NT, third_component, 0, unroll=3)
    for m, (dt, ds) in zip(mb, DIRS):
        there(-ds, m.wait_recv)

    def keep(x, rows):
        return jnp.where((row128 >= rows[0]) & (row128 < rows[1]), x, 0.0)

    def turn(x, by, axis):
        return pltpu.roll(x, by % x.shape[axis], axis) if by % x.shape[axis] else x

    def rows_of(ot):
        return (2, 4) if ot == -2 else (0, 2) if ot == 2 else (0, 4)

    def diag_rows(x, ot):
        return turn(keep(x, (1, 2) if ot == -2 else (0, 1) if ot == 2 else (0, 2)), 3 + 2 * ot, 0)

    near = [(0, bsend)] + [(-dt, brecv.at[i]) for i, (dt, ds) in enumerate(DIRS) if ds == 0]
    d0 = sum(diag_rows(ref[40:48, :], ot) for ot, ref in near)
    beside = []
    for sent in (1, -1):
        got = [(-dt, precv[i - 4]) for i, (dt, ds) in enumerate(DIRS) if ds == sent]
        beside.append((
            sum(turn(keep(x, rows_of(ot)), 2 * ot + 2, 0) for ot, x in got),
            sum(turn(keep(x, (rows_of(ot)[0] + 4, rows_of(ot)[1] + 4)), 2 * ot + 6, 0) for ot, x in got),
            sum(diag_rows(x, ot) for ot, x in got)))
    s_near = sum(turn(keep(ref[40:48, :], (rows_of(ot)[0] + 4, rows_of(ot)[1] + 4)), 2 * ot + 6, 0)
                 for ot, ref in near)
    (ml, sl, dl), (mr, sr, dr) = beside
    from_left, from_right = lane128 >= 125, lane128 <= 2
    d1 = (jnp.where(from_left, turn(dl, -43, 1), 0.0) + jnp.where(from_right, turn(dr, -41, 1), 0.0))
    ok = jnp.where(lane128 >= 64, (s > 0).astype(F32), (s < n_span - 1).astype(F32))
    inv = jnp.concatenate([0.8 / (4.0 + d0), ok * 0.8 / (4.0 + d1)], 1)
    for n in range(NT):
        lo4 = 4 * (n % 2)
        r0 = sum(turn(keep(ref[8 * (n // 2):8 * (n // 2) + 8, :], (rows_of(ot)[0] + lo4, rows_of(ot)[1] + lo4)),
                      2 * ot + 2 - lo4, 0) for ot, ref in near)
        r0 = r0 + jnp.where(lane128 == 0, turn(sl, -(3 + 4 * n), 1), 0.0)
        r0 = r0 + jnp.where(lane128 == 127, turn(sr, -(1 + 4 * n), 1), 0.0)
        r1 = jnp.where((lane128 == 0) | (lane128 == 127), turn(s_near, -(1 + 2 * n), 1), 0.0)
        r1 = r1 + jnp.where(from_left, turn(ml, -(3 + 4 * n), 1), 0.0)
        r1 = r1 + jnp.where(from_right, turn(mr, -(1 + 4 * n), 1), 0.0)
        rhs = jnp.concatenate([r0, r1], 1)
        x = inv * rhs
        for _ in range(CSWEEPS - 1):
            around = (pltpu.roll(x, 1, 0) + pltpu.roll(x, 7, 0)
                      + pltpu.roll(x, 1, 1) + pltpu.roll(x, 255, 1))
            x = 0.2 * x + inv * (rhs + around)
        mine = jnp.where(row128 < 4, x[3:4, 0:128], x[4:5, 0:128])
        top = mine.astype(BF16).astype(F32)
        lhs[n * 8:n * 8 + 8, :] = jnp.concatenate([top, mine - top], 1)

    for m in m1 + m2 + m3:
        m.wait_send()
    for m, ds in list(zip(ms, (1, -1))) + [(m, d[1]) for m, d in zip(md, DIAG)] + [
            (m, d[1]) for m, d in zip(mb, DIRS)]:
        there(ds, m.wait_send)


def lift_kernel(live_ref, raw_ref, sm_ref, lhs, own_hbm, pred_hbm, corr_hbm, own_ref, corr, sems):
    cells = own_ref.shape[1]
    width = 256
    count = cells // width
    pred_out = pltpu.make_async_copy(raw_ref, pred_hbm, sems.at[0])
    pred_out.start()
    own_in = pltpu.make_async_copy(own_hbm, own_ref, sems.at[1])
    own_in.start()
    first = lax.axis_index("span") * (cells // FAN)
    x = lhs[...].astype(BF16)
    own_in.wait()
    live = live_ref[0, 0]
    outs = []
    for j in range(count):
        at = slice(j * width, j * width + width)
        r = lax.broadcasted_iota(jnp.int32, (256, width), 1) + j * width
        k = lax.broadcasted_iota(jnp.int32, (256, width), 0) & 127
        b = r >> 4
        e = r & (FAN - 1)
        to = jnp.where(e == 0, b - 1, jnp.where(e == FAN - 1, b + 1, -9))
        l1 = jnp.dot(x, (b == k).astype(F32).astype(BF16), preferred_element_type=F32)
        l2 = jnp.dot(x, (to == k).astype(F32).astype(BF16), preferred_element_type=F32)
        r = lax.broadcasted_iota(jnp.int32, (8, width), 1) + j * width
        f = (r < live * (cells // BLOCKS)).astype(F32)
        away = own_ref[:, at] != first + (r >> 4)
        for n in range(NT):
            k = slice(n * 8, n * 8 + 8)
            corr[k, at] = f * (sm_ref[k, at] + jnp.where(away, l2[k], l1[k]))
        if j % 2:
            at = slice(j * width - width, j * width + width)
            outs.append(pltpu.make_async_copy(corr.at[:, at], corr_hbm.at[:, at], sems.at[2 + j // 2]))
            outs[-1].start()
    for m in outs + [pred_out]:
        m.wait()


def shards(n_theta, n_span, velocity, pressure, diffusivity, live_blocks, owner_map, coarse_diag):
    ncomp, ntime, planes, cells = velocity.shape
    vmem = pl.BlockSpec(memory_space=pltpu.VMEM)
    hbm = pl.BlockSpec(memory_space=pltpu.HBM)
    smem = pl.BlockSpec(memory_space=pltpu.SMEM)
    n = len(DIRS)
    rows = ntime * planes
    pin = lambda x: pltpu.with_memory_space_constraint(x, pltpu.HBM)
    own, live = pin(owner_map), live_blocks
    raw, sm, lhs = pl.pallas_call(
        functools.partial(kernel, n_theta, n_span),
        out_shape=(
            jax.ShapeDtypeStruct((ncomp * rows, cells), F32),
            jax.ShapeDtypeStruct((rows, cells), F32),
            jax.ShapeDtypeStruct((rows, 256), F32),
        ),
        in_specs=[smem] + [hbm] * 5,
        out_specs=(vmem, vmem, vmem),
        scratch_shapes=[
            pltpu.VMEM((ncomp * rows, cells), F32),
            pltpu.VMEM((rows, cells), F32),
            pltpu.VMEM((planes, cells), F32),
            pltpu.VMEM((planes, cells), jnp.int32),
            pltpu.VMEM(coarse_diag.shape, F32),
            pltpu.VMEM((2, 48, cells), F32),
            pltpu.VMEM((2, 48, cells), F32),
            pltpu.VMEM((2, 72, 128), F32),
            pltpu.VMEM((2, 72, 128), F32),
            pltpu.VMEM((4, 16, 128), F32),
            pltpu.VMEM((4, 16, 128), F32),
            pltpu.VMEM((48, 128), F32),
            pltpu.VMEM((4, 48, 128), F32),
            pltpu.VMEM((2, 8, 128), F32),
            pltpu.VMEM((10, 8, 128), F32),
            pltpu.VMEM((72, 128), F32),
            pltpu.VMEM((208, cells), BF16),
            pltpu.VMEM((208, cells), BF16),
            pltpu.VMEM((128, cells), BF16),
            pltpu.VMEM((128, cells), BF16),
            pltpu.VMEM((2, 9, cells), F32),
            pltpu.SemaphoreType.DMA((12 + n,)),
            pltpu.SemaphoreType.DMA((12 + n,)),
            pltpu.SemaphoreType.DMA((7,)),
        ],
        compiler_params=pltpu.CompilerParams(
            collective_id=0, has_side_effects=True, vmem_limit_bytes=40 * 2**20),
    )(
        live,
        pin(velocity.reshape(ncomp * rows, cells)),
        pin(pressure.reshape(rows, cells)),
        pin(diffusivity), own, pin(coarse_diag),
    )
    pred, corr = pl.pallas_call(
        lift_kernel,
        out_shape=(
            jax.ShapeDtypeStruct((ncomp * rows, cells), F32),
            jax.ShapeDtypeStruct((rows, cells), F32),
        ),
        in_specs=[smem, vmem, vmem, vmem, hbm],
        out_specs=(hbm, hbm),
        scratch_shapes=[
            pltpu.VMEM((planes, cells), jnp.int32),
            pltpu.VMEM((rows, cells), F32),
            pltpu.SemaphoreType.DMA((8,)),
        ],
        compiler_params=pltpu.CompilerParams(vmem_limit_bytes=24 * 2**20),
    )(live, raw, sm, lhs, own)
    return pred.reshape(velocity.shape), corr.reshape(pressure.shape)


def solution(mesh):
    return jax.shard_map(
        functools.partial(shards, mesh.shape["theta"], mesh.shape["span"]),
        mesh=mesh,
        in_specs=(
            P(None, None, "theta", "span"),
            P(None, "theta", "span"),
            P("theta", "span"),
            P("theta", "span"),
            P("theta", "span"),
            P("theta", "span"),
        ),
        out_specs=(P(None, None, "theta", "span"), P(None, "theta", "span")),
        check_vma=False,
    )
```

```python
import functools
import math

import jax
import jax.numpy as jnp
import numpy as np
from jax import lax
from jax.experimental import pallas as pl
from jax.experimental.pallas import tpu as pltpu
from jax.sharding import PartitionSpec as P

MESH = pl.DeviceIdType.MESH
BLOCKS = 8
CSWEEPS = 4
NT = 9
FAN = 16
F32 = jnp.float32
BF16 = jnp.bfloat16

DIRS = [(1, 0), (-1, 0), (2, 0), (-2, 0)] + [
    (dt, ds) for ds in (1, -1) for dt in (0, 1, -1, 2, -2)
]
NEAR = [(dt, ds) for dt in (0, 1, -1) for ds in (0, 1, -1) if dt or ds]
DIAG = [(1, 1), (1, -1), (-1, 1), (-1, -1)]
FREQ = [0.15 * (-1.0) ** d / math.sin(math.pi * d / NT) for d in range(1, 5)]


def kernel(
    n_theta, n_span,
    live_ref, v_hbm, p_hbm, d_hbm, own_hbm, cd_hbm,
    pred_ref, sm_ref, lhs,
    v_ref, p_ref, d_ref, own_ref, cd_ref,
    tsend, trecv, ssend, srecv, dsend, drecv, bsend, brecv,
    psend, precv, side_ref, stay, moved, st1, st2, edge0,
    send_sem, recv_sem, load_sem,
):
    cells = v_ref.shape[1]
    cols = cells // FAN
    t, s = lax.axis_index("theta"), lax.axis_index("span")
    third = NT * 8
    loads = [pltpu.make_async_copy(v_hbm.at[third * c:third * c + third], v_ref.at[third * c:third * c + third],
                                   load_sem.at[c]) for c in range(3)]
    loads += [pltpu.make_async_copy(a, b, load_sem.at[3 + i]) for i, (a, b) in enumerate((
        (p_hbm, p_ref), (d_hbm, d_ref), (own_hbm, own_ref), (cd_hbm, cd_ref)))]
    for m in loads:
        m.start()
    tile = lambda i: pl.ds(pl.multiple_of(i * 8, 8), 8)

    def peer(dt, ds):
        return (lax.rem(t + dt + n_theta, n_theta), s + ds)

    def there(ds, act):
        if ds == 0:
            act()
        elif ds > 0:
            pl.when(s < n_span - 1)(act)
        else:
            pl.when(s > 0)(act)

    def remote(src, dst, slot, dt, ds):
        return pltpu.make_async_remote_copy(
            src_ref=src, dst_ref=dst, send_sem=send_sem.at[slot], recv_sem=recv_sem.at[slot],
            device_id=peer(dt, ds), device_id_type=MESH)

    barrier = pltpu.get_barrier_semaphore()
    for dt, ds in NEAR:
        there(ds, lambda dt=dt, ds=ds: pl.semaphore_signal(
            barrier, inc=1, device_id=peer(dt, ds), device_id_type=MESH))

    lane = lax.broadcasted_iota(jnp.int32, (1, cells), 1)
    row8 = lax.broadcasted_iota(jnp.int32, (8, 1), 0)
    lane128 = lax.broadcasted_iota(jnp.int32, (8, 128), 1)
    row128 = lax.broadcasted_iota(jnp.int32, (8, 128), 0)
    for m in loads:
        m.wait()
    fl = (lane < live_ref[0, 0] * (cells // BLOCKS)).astype(F32)
    base = s * cols + (lane >> 4)
    mv = (own_ref[...] != base).astype(F32)
    df = d_ref[...] * (0.1 * fl)

    def pack(way, row, ref, plane, count, first=0):
        for i in range(count):
            at = 8 * (first + i) + plane
            tsend[way, row + i:row + i + 1, :] = ref[at:at + 1, :]

    for way, plane in ((0, 7), (1, 0)):
        pack(way, 0, v_ref, plane, 18)
        pack(way, 18, p_ref, plane, 9)
        pack(way, 39, v_ref, plane, 9, 18)
        tsend[way, 27:28, :] = df[plane:plane + 1, :]
        tsend[way, 28:29, :] = mv[plane:plane + 1, :]
        tsend[way, 29:30, :] = fl
    for i, (dt, ds) in enumerate(DIAG):
        way = 0 if dt > 0 else 1
        c0 = cells - 128 if ds > 0 else 0
        at = 127 if ds > 0 else 0
        a0 = tsend[way, 0:9, c0:c0 + 128][:, at:at + 1]
        a1 = tsend[way, 9:18, c0:c0 + 128][:, at:at + 1]
        l9 = lax.broadcasted_iota(jnp.int32, (9, 128), 1)
        dsend[i, 0:9, :] = jnp.where(l9 == 0, a0, a1)

    pl.semaphore_wait(barrier, jnp.where((s > 0) & (s < n_span - 1), 8, 5))

    m1 = [remote(tsend.at[w, 0:24], trecv.at[w, 0:24], w, 1 - 2 * w, 0) for w in range(2)]
    m2 = [remote(tsend.at[w, 24:40], trecv.at[w, 24:40], 2 + w, 1 - 2 * w, 0) for w in range(2)]
    last = 10 + len(DIRS)
    m3 = [remote(tsend.at[w, 40:48], trecv.at[w, 40:48], last + w, 1 - 2 * w, 0) for w in range(2)]
    ms = [remote(ssend.at[w], srecv.at[w], 4 + w, 0, 1 - 2 * w) for w in range(2)]
    md = [remote(dsend.at[i], drecv.at[i], 6 + i, dt, ds) for i, (dt, ds) in enumerate(DIAG)]
    mb = [remote(bsend, brecv.at[i], 10 + i, dt, ds) if ds == 0 else
          remote(psend.at[(1 - ds) // 2], precv.at[i - 4], 10 + i, dt, ds)
          for i, (dt, ds) in enumerate(DIRS)]
    for m in m1:
        m.start()
    for m, (dt, ds) in zip(md, DIAG):
        there(ds, m.start)

    def clear(ds):
        w = 0 if ds < 0 else 1
        srecv[w] = jnp.zeros(srecv.shape[1:], F32)
        for i, (_, e) in enumerate(DIAG):
            if e == -ds:
                drecv[i] = jnp.zeros(drecv.shape[1:], F32)
        for i, (_, e) in enumerate(DIRS):
            if e == -ds:
                precv[i - 4] = jnp.zeros(precv.shape[1:], F32)

    pl.when(s == 0)(lambda: clear(-1))
    pl.when(s == n_span - 1)(lambda: clear(1))

    def a_pair(x):
        return (jnp.where(row8 == 7, 0.0, pltpu.roll(x, 7, 0)),
                jnp.where(row8 == 0, 0.0, pltpu.roll(x, 1, 0)))

    def r_pair(x):
        return (jnp.where(lane == cells - 1, 0.0, pltpu.roll(x, cells - 1, 1)),
                jnp.where(lane == 0, 0.0, pltpu.roll(x, 1, 1)))

    width = 256
    for c in range(3):
        def source(j, _):
            at = pl.ds(pl.multiple_of(j * width, width), width)
            x = [v_ref[(c * NT + n) * 8:(c * NT + n) * 8 + 8, at] for n in range(NT)]
            acc = list(x)
            for d in range(1, 5):
                for n in range(NT):
                    gap = (x[(n - d) % NT] - x[(n + d) % NT]) * (0.2 * FREQ[d - 1])
                    acc[n] = acc[n] - gap
            for n in range(NT):
                pred_ref[(c * NT + n) * 8:(c * NT + n) * 8 + 8, at] = acc[n]
            return 0

        lax.fori_loop(0, cells // width, source, 0)

        def local(n, _):
            x = v_ref[tile(c * NT + n), :]
            ap, am = a_pair(x)
            rp, rm = r_pair(x)
            out = pred_ref[tile(c * NT + n), :] - 0.1 * (x - am)
            if c < 2:
                q = p_ref[tile(n), :]
                qp, qm = a_pair(q) if c == 0 else r_pair(q)
                out = out - 0.1 * (qp - qm)
            pred_ref[tile(c * NT + n), :] = fl * out + df * (ap + am + rp + rm - 4.0 * x)
            return 0

        lax.fori_loop(0, NT, local, 0)

        if c == 0:
            for way, plane in ((0, 7), (1, 0)):
                pack(way, 30, pred_ref, plane, 9)
                m2[way].start()
        if c == 1:
            def columns(n, _):
                for way in range(2):
                    c0, at = (cells - 128, 127) if way == 0 else (0, 0)
                    got = jnp.zeros((8, 128), F32)
                    for f, x in enumerate((
                        v_ref[tile(n), c0:c0 + 128], v_ref[tile(NT + n), c0:c0 + 128],
                        v_ref[tile(2 * NT + n), c0:c0 + 128], p_ref[tile(n), c0:c0 + 128],
                        pred_ref[tile(NT + n), c0:c0 + 128], df[:, c0:c0 + 128],
                        jnp.broadcast_to(fl[:, c0:c0 + 128], (8, 128)))):
                        got = jnp.where(lane128 == f, x[:, at:at + 1], got)
                    ssend[way, tile(n), :] = got
                return 0

            lax.fori_loop(0, NT, columns, 0)
            for m, ds in zip(ms, (1, -1)):
                there(ds, m.start)

    def members(j, _):
        at = pl.ds(pl.multiple_of(j * width, width), width)
        r = lax.broadcasted_iota(jnp.int32, (128, width), 1) + j * width
        k = lax.broadcasted_iota(jnp.int32, (128, width), 0)
        b = r >> 4
        e = r & (FAN - 1)
        to = jnp.where(e == 0, b - 1, jnp.where(e == FAN - 1, b + 1, -9))
        st1[:, at] = (b == k).astype(F32).astype(BF16)
        st2[:, at] = (to == k).astype(F32).astype(BF16)
        return 0

    lax.fori_loop(0, cells // width, members, 0)

    for m in m1:
        m.wait_recv()
    for m, (dt, ds) in zip(md, DIAG):
        there(-ds, m.wait_recv)
    for m, ds in zip(ms, (1, -1)):
        there(-ds, m.wait_recv)
    w_dn = jnp.where(row8 == 0, df + 0.1 * fl, 0.0)
    w_up = jnp.where(row8 == 7, df, 0.0)
    q_dn = jnp.where(row8 == 0, 0.1 * fl, 0.0)
    q_up = jnp.where(row8 == 7, 0.1 * fl, 0.0)

    def completed(n, c, left, right):
        i = c * NT + n
        halo = pl.ds(i if c < 2 else 39 + n, 1)
        out = pred_ref[tile(i), :] + w_dn * trecv[0, halo, :] + w_up * trecv[1, halo, :]
        if c == 0:
            out = (out + q_dn * trecv[0, pl.ds(18 + n, 1), :]
                   - q_up * trecv[1, pl.ds(18 + n, 1), :])
        ends = []
        for c0, col, side, sign in ((0, 0, left, 0.1), (cells - 128, 127, right, -0.1)):
            at = slice(c0, c0 + 128)
            x = df[:, at] * side[:, c:c + 1]
            if c == 1:
                x = x + sign * fl[:, at] * side[:, 3:4]
            ends.append(out[:, at] + jnp.where(lane128 == col, x, 0.0))
        out = jnp.concatenate([ends[0], out[:, 128:cells - 128], ends[1]], 1)
        pred_ref[tile(i), :] = out
        return out

    def second_component(n, _):
        completed(n, 1, srecv[0, tile(n), :], srecv[1, tile(n), :])
        return 0

    lax.fori_loop(0, NT, second_component, 0, unroll=3)
    for m in m2:
        m.wait_recv()
    for m in m3:
        m.start()

    df_dn, fl_dn = trecv[0, 27:28, :], trecv[0, 29:30, :]
    df_up, fl_up = trecv[1, 27:28, :], trecv[1, 29:30, :]
    lo, hi = lane == 0, lane == cells - 1
    edge0[0] = (trecv[0, 30:39, :] + df_dn * tsend[1, 0:9, :] - 0.1 * fl_dn * tsend[1, 18:27, :]
                + jnp.where(lo, df_dn * drecv[0, 0:9, 0:1], 0.0)
                + jnp.where(hi, df_dn * drecv[1, 0:9, 0:1], 0.0))
    edge0[1] = (trecv[1, 30:39, :] + (df_up + 0.1 * fl_up) * tsend[0, 0:9, :]
                + 0.1 * fl_up * tsend[0, 18:27, :]
                + jnp.where(lo, df_up * drecv[2, 0:9, 0:1], 0.0)
                + jnp.where(hi, df_up * drecv[3, 0:9, 0:1], 0.0))

    def complete(n, _):
        left, right = srecv[0, tile(n), :], srecv[1, tile(n), :]
        first = completed(n, 0, left, right)
        second = pred_ref[tile(NT + n), :]
        fp = jnp.where(row8 == 7, edge0[1, pl.ds(n, 1), :], pltpu.roll(first, 7, 0))
        fm = jnp.where(row8 == 0, edge0[0, pl.ds(n, 1), :], pltpu.roll(first, 1, 0))
        x = [v_ref[tile(NT + n), 0:128][:, 0:1],
             v_ref[tile(NT + n), cells - 128:cells][:, 127:128]]
        q = [p_ref[tile(n), 0:128][:, 0:1], p_ref[tile(n), cells - 128:cells][:, 127:128]]
        rows = pl.ds(n, 1)

        def corner(side, dn, up):
            return (jnp.where(row8 == 0, (side[:, 5:6] + 0.1 * side[:, 6:7]) * drecv[dn, rows, :][:, 1:2], 0.0)
                    + jnp.where(row8 == 7, side[:, 5:6] * drecv[up, rows, :][:, 1:2], 0.0))

        pl1 = (left[:, 4:5] + left[:, 5:6] * x[0] - 0.1 * left[:, 6:7] * q[0]
               + corner(left, 0, 2))
        pr1 = (right[:, 4:5] + right[:, 5:6] * x[1] + 0.1 * right[:, 6:7] * q[1]
               + corner(right, 1, 3))
        sp = jnp.where(hi, pr1, pltpu.roll(second, cells - 1, 1))
        sn = jnp.where(lo, pl1, pltpu.roll(second, 1, 1))
        sm = 0.1 * fl * (fp - fm + sp - sn)
        sm_ref[tile(n), :] = sm
        ap, am = a_pair(sm)
        rp, rm = r_pair(sm)
        rem = fl * (sm + (ap + am + rp + rm))
        gone = rem * mv
        kept = rem - gone
        at = pl.ds(pl.multiple_of(n * 16, 16), 16)
        for ref, x in ((stay, kept), (moved, gone)):
            top = x.astype(BF16).astype(F32)
            ref[at, :] = jnp.concatenate([top, x - top], 0).astype(BF16)
        e = jnp.where(lane128 == 0, sm[:, cells - 1:cells],
                      jnp.where(lane128 == 127, sm[:, 0:1] * left[:, 6:7], 0.0))
        e0 = jnp.sum(e[0:4], axis=0, keepdims=True)
        e1 = jnp.sum(e[4:8], axis=0, keepdims=True)
        side_ref[tile(n), :] = jnp.where(row128 == 5, e0, jnp.where(row128 == 6, e1, 0.0))
        return 0

    lax.fori_loop(0, NT, complete, 0, unroll=3)

    def pieces(x):
        top = x.astype(BF16).astype(F32)
        return [top, x - top]

    zero7 = jnp.zeros((7, cells), F32)
    kept, gone = [], []
    for w, plane in ((0, 0), (1, 7)):
        x = jnp.concatenate([sm_ref[8 * i + plane:8 * i + plane + 1, :] for i in range(NT)], 0)
        x = x * trecv[w, 29:30, :]
        g = x * trecv[w, 28:29, :]
        for rows, y in ((kept, x - g), (gone, g)):
            for z in pieces(y):
                rows += [z, zero7]
    for ref, rows in ((stay, kept), (moved, gone)):
        for i in range(4):
            at = 16 * NT + 16 * i
            ref[at:at + 16, :] = jnp.concatenate(rows[2 * i:2 * i + 2], 0).astype(BF16)

    nt = (((1,), (1,)), ((), ()))
    tot = (lax.dot_general(stay[...], st1[...], nt, preferred_element_type=F32)
           + lax.dot_general(moved[...], st2[...], nt, preferred_element_type=F32))
    e_dn = tot[16 * NT:16 * NT + 16] + tot[16 * NT + 16:16 * NT + 32]
    e_up = tot[16 * NT + 32:16 * NT + 48] + tot[16 * NT + 48:16 * NT + 64]
    pack_r, pack_l = jnp.zeros((8, 128), F32), jnp.zeros((8, 128), F32)
    main, sides = [], jnp.zeros((8, 128), F32)
    for n in range(NT):
        x = tot[16 * n:16 * n + 8] + tot[16 * n + 8:16 * n + 16]
        x0 = jnp.sum(x[0:4], axis=0, keepdims=True)
        x1 = jnp.sum(x[4:8], axis=0, keepdims=True)
        x = jnp.where(row128 == 0, e_dn[n:n + 1], jnp.where(row128 == 1, x0, jnp.where(
            row128 == 2, x1, jnp.where(row128 == 3, e_up[n:n + 1], side_ref[n * 8:n * 8 + 8, :]))))
        main.append(x)
        slot = (lane128 >> 2) == n
        pack_r = jnp.where(slot, pltpu.roll(x, 3 + 4 * n, 1), pack_r)
        pack_l = jnp.where(slot, pltpu.roll(x, 1 + 4 * n, 1), pack_l)
        sides = jnp.where((lane128 >> 1) == n, pltpu.roll(x, 1 + 2 * n, 1), sides)
    cd = jnp.concatenate([cd_ref[...], jnp.zeros((6, 128), F32)], 0)
    for i in range(5):
        y = main[2 * i + 1] if 2 * i + 1 < NT else jnp.zeros((8, 128), F32)
        bsend[8 * i:8 * i + 8, :] = jnp.where(row128 < 4, main[2 * i], pltpu.roll(y, 4, 0))
    bsend[40:48, :] = jnp.where(row128 < 4, cd, sides)
    cslot = (lane128 >> 2) == 10
    psend[0] = jnp.where(cslot, pltpu.roll(cd, 43, 1), pack_r)
    psend[1] = jnp.where(cslot, pltpu.roll(cd, 41, 1), pack_l)
    for m, (dt, ds) in sorted(zip(mb, DIRS), key=lambda x: -abs(x[1][0]) - abs(x[1][1])):
        there(ds, m.start)

    def third_component(n, _):
        completed(n, 2, srecv[0, tile(n), :], srecv[1, tile(n), :])
        return 0

    for m in m3:
        m.wait_recv()
    lax.fori_loop(0, NT, third_component, 0, unroll=3)
    for m, (dt, ds) in zip(mb, DIRS):
        there(-ds, m.wait_recv)

    def keep(x, rows):
        return jnp.where((row128 >= rows[0]) & (row128 < rows[1]), x, 0.0)

    def turn(x, by, axis):
        return pltpu.roll(x, by % x.shape[axis], axis) if by % x.shape[axis] else x

    def rows_of(ot):
        return (2, 4) if ot == -2 else (0, 2) if ot == 2 else (0, 4)

    def diag_rows(x, ot):
        return turn(keep(x, (1, 2) if ot == -2 else (0, 1) if ot == 2 else (0, 2)), 3 + 2 * ot, 0)

    near = [(0, bsend)] + [(-dt, brecv.at[i]) for i, (dt, ds) in enumerate(DIRS) if ds == 0]
    d0 = sum(diag_rows(ref[40:48, :], ot) for ot, ref in near)
    beside = []
    for sent in (1, -1):
        got = [(-dt, precv[i - 4]) for i, (dt, ds) in enumerate(DIRS) if ds == sent]
        beside.append((
            sum(turn(keep(x, rows_of(ot)), 2 * ot + 2, 0) for ot, x in got),
            sum(turn(keep(x, (rows_of(ot)[0] + 4, rows_of(ot)[1] + 4)), 2 * ot + 6, 0) for ot, x in got),
            sum(diag_rows(x, ot) for ot, x in got)))
    s_near = sum(turn(keep(ref[40:48, :], (rows_of(ot)[0] + 4, rows_of(ot)[1] + 4)), 2 * ot + 6, 0)
                 for ot, ref in near)
    (ml, sl, dl), (mr, sr, dr) = beside
    from_left, from_right = lane128 >= 125, lane128 <= 2
    d1 = (jnp.where(from_left, turn(dl, -43, 1), 0.0) + jnp.where(from_right, turn(dr, -41, 1), 0.0))
    ok = jnp.where(lane128 >= 64, (s > 0).astype(F32), (s < n_span - 1).astype(F32))
    inv = jnp.concatenate([0.8 / (4.0 + d0), ok * 0.8 / (4.0 + d1)], 1)
    for n in range(NT):
        lo4 = 4 * (n % 2)
        r0 = sum(turn(keep(ref[8 * (n // 2):8 * (n // 2) + 8, :], (rows_of(ot)[0] + lo4, rows_of(ot)[1] + lo4)),
                      2 * ot + 2 - lo4, 0) for ot, ref in near)
        r0 = r0 + jnp.where(lane128 == 0, turn(sl, -(3 + 4 * n), 1), 0.0)
        r0 = r0 + jnp.where(lane128 == 127, turn(sr, -(1 + 4 * n), 1), 0.0)
        r1 = jnp.where((lane128 == 0) | (lane128 == 127), turn(s_near, -(1 + 2 * n), 1), 0.0)
        r1 = r1 + jnp.where(from_left, turn(ml, -(3 + 4 * n), 1), 0.0)
        r1 = r1 + jnp.where(from_right, turn(mr, -(1 + 4 * n), 1), 0.0)
        rhs = jnp.concatenate([r0, r1], 1)
        x = inv * rhs
        for _ in range(CSWEEPS - 1):
            around = (pltpu.roll(x, 1, 0) + pltpu.roll(x, 7, 0)
                      + pltpu.roll(x, 1, 1) + pltpu.roll(x, 255, 1))
            x = 0.2 * x + inv * (rhs + around)
        mine = jnp.where(row128 < 4, x[3:4, 0:128], x[4:5, 0:128])
        top = mine.astype(BF16).astype(F32)
        lhs[n * 8:n * 8 + 8, :] = jnp.concatenate([top, mine - top], 1)

    for m in m1 + m2 + m3:
        m.wait_send()
    for m, ds in list(zip(ms, (1, -1))) + [(m, d[1]) for m, d in zip(md, DIAG)] + [
            (m, d[1]) for m, d in zip(mb, DIRS)]:
        there(ds, m.wait_send)


def lift_kernel(live_ref, raw_ref, sm_ref, lhs, own_hbm, pred_hbm, corr_hbm, own_ref, corr, sems):
    cells = own_ref.shape[1]
    width = 256
    count = cells // width
    piece = raw_ref.shape[0] // 3
    pred_out = [pltpu.make_async_copy(raw_ref.at[piece * c:piece * c + piece], pred_hbm.at[piece * c:piece * c + piece],
                                      sems.at[6 + c]) for c in range(3)]
    for m in pred_out:
        m.start()
    own_in = pltpu.make_async_copy(own_hbm, own_ref, sems.at[1])
    own_in.start()
    first = lax.axis_index("span") * (cells // FAN)
    x = lhs[...].astype(BF16)
    own_in.wait()
    live = live_ref[0, 0]
    outs = []
    for j in range(count):
        at = slice(j * width, j * width + width)
        r = lax.broadcasted_iota(jnp.int32, (256, width), 1) + j * width
        k = lax.broadcasted_iota(jnp.int32, (256, width), 0) & 127
        b = r >> 4
        e = r & (FAN - 1)
        to = jnp.where(e == 0, b - 1, jnp.where(e == FAN - 1, b + 1, -9))
        l1 = jnp.dot(x, (b == k).astype(F32).astype(BF16), preferred_element_type=F32)
        l2 = jnp.dot(x, (to == k).astype(F32).astype(BF16), preferred_element_type=F32)
        r = lax.broadcasted_iota(jnp.int32, (8, width), 1) + j * width
        f = (r < live * (cells // BLOCKS)).astype(F32)
        away = own_ref[:, at] != first + (r >> 4)
        for n in range(NT):
            k = slice(n * 8, n * 8 + 8)
            corr[k, at] = f * (sm_ref[k, at] + jnp.where(away, l2[k], l1[k]))
        if j % 2:
            at = slice(j * width - width, j * width + width)
            outs.append(pltpu.make_async_copy(corr.at[:, at], corr_hbm.at[:, at], sems.at[2 + j // 2]))
            outs[-1].start()
    for m in outs + pred_out:
        m.wait()


def shards(n_theta, n_span, velocity, pressure, diffusivity, live_blocks, owner_map, coarse_diag):
    ncomp, ntime, planes, cells = velocity.shape
    vmem = pl.BlockSpec(memory_space=pltpu.VMEM)
    hbm = pl.BlockSpec(memory_space=pltpu.HBM)
    smem = pl.BlockSpec(memory_space=pltpu.SMEM)
    n = len(DIRS)
    rows = ntime * planes
    pin = lambda x: pltpu.with_memory_space_constraint(x, pltpu.HBM)
    own, live = pin(owner_map), live_blocks
    raw, sm, lhs = pl.pallas_call(
        functools.partial(kernel, n_theta, n_span),
        out_shape=(
            jax.ShapeDtypeStruct((ncomp * rows, cells), F32),
            jax.ShapeDtypeStruct((rows, cells), F32),
            jax.ShapeDtypeStruct((rows, 256), F32),
        ),
        in_specs=[smem] + [hbm] * 5,
        out_specs=(vmem, vmem, vmem),
        scratch_shapes=[
            pltpu.VMEM((ncomp * rows, cells), F32),
            pltpu.VMEM((rows, cells), F32),
            pltpu.VMEM((planes, cells), F32),
            pltpu.VMEM((planes, cells), jnp.int32),
            pltpu.VMEM(coarse_diag.shape, F32),
            pltpu.VMEM((2, 48, cells), F32),
            pltpu.VMEM((2, 48, cells), F32),
            pltpu.VMEM((2, 72, 128), F32),
            pltpu.VMEM((2, 72, 128), F32),
            pltpu.VMEM((4, 16, 128), F32),
            pltpu.VMEM((4, 16, 128), F32),
            pltpu.VMEM((48, 128), F32),
            pltpu.VMEM((4, 48, 128), F32),
            pltpu.VMEM((2, 8, 128), F32),
            pltpu.VMEM((10, 8, 128), F32),
            pltpu.VMEM((72, 128), F32),
            pltpu.VMEM((208, cells), BF16),
            pltpu.VMEM((208, cells), BF16),
            pltpu.VMEM((128, cells), BF16),
            pltpu.VMEM((128, cells), BF16),
            pltpu.VMEM((2, 9, cells), F32),
            pltpu.SemaphoreType.DMA((12 + n,)),
            pltpu.SemaphoreType.DMA((12 + n,)),
            pltpu.SemaphoreType.DMA((7,)),
        ],
        compiler_params=pltpu.CompilerParams(
            collective_id=0, has_side_effects=True, vmem_limit_bytes=40 * 2**20),
    )(
        live,
        pin(velocity.reshape(ncomp * rows, cells)),
        pin(pressure.reshape(rows, cells)),
        pin(diffusivity), own, pin(coarse_diag),
    )
    pred, corr = pl.pallas_call(
        lift_kernel,
        out_shape=(
            jax.ShapeDtypeStruct((ncomp * rows, cells), F32),
            jax.ShapeDtypeStruct((rows, cells), F32),
        ),
        in_specs=[smem, vmem, vmem, vmem, hbm],
        out_specs=(hbm, hbm),
        scratch_shapes=[
            pltpu.VMEM((planes, cells), jnp.int32),
            pltpu.VMEM((rows, cells), F32),
            pltpu.SemaphoreType.DMA((9,)),
        ],
        compiler_params=pltpu.CompilerParams(vmem_limit_bytes=24 * 2**20),
    )(live, raw, sm, lhs, own)
    return pred.reshape(velocity.shape), corr.reshape(pressure.shape)


def solution(mesh):
    return jax.shard_map(
        functools.partial(shards, mesh.shape["theta"], mesh.shape["span"]),
        mesh=mesh,
        in_specs=(
            P(None, None, "theta", "span"),
            P(None, "theta", "span"),
            P("theta", "span"),
            P("theta", "span"),
            P("theta", "span"),
            P("theta", "span"),
        ),
        out_specs=(P(None, None, "theta", "span"), P(None, "theta", "span")),
        check_vma=False,
    )
```
